32 devices in a mesh: members: 2 (over y), lon: 4 (over z), lat: 2 (over x), lev: 2 (over core).
Axes of the slice: x: 2, y: 2, z: 4, core: 2. Of those that a mesh axis runs over, the one named last changes fastest.
Arguments:
- tracers: float32 [4, 6, 256, 512], P('members', 'lev', 'lat', 'lon'), parts along dimension 0, may hold values from -12 to 12
- land_sea: int32 [6, 256, 512], P('lev', 'lat', 'lon'), may hold values 0 or 1
- faces_east: float32 [6, 6, 256, 512], P('members', 'lev', 'lat', 'lon'), parts along dimension 0, may hold values from -1 to 1, as said below
- faces_north: float32 [6, 6, 256, 512], P('members', 'lev', 'lat', 'lon'), parts along dimension 0, may hold values from -1 to 1, as said below
Outputs:
- advanced: float32 [4, 6, 256, 512], P('members', 'lev', 'lat', 'lon'), parts along dimension 0
The draws below stay inside these ranges and needn't reach their ends.
There are 2 independent parts, one for each index of `members`. The reference program is written for one: setup_inputs(seed, part) draws one part's arguments, and reference() takes and returns one part's arrays. A program takes and returns all parts, laid end to end along the dimension named above; an argument that names none is the same for every part. Nothing has to cross between parts.
Inputs may be any that keep to these rules, and one draw needn't show every extreme that they name: `faces_east`: plane 0 lies in -0.25 to 0.25, plane 1 in 0.02 to 0.1, plane 2 in -1 to 1. `faces_north`: plane 0 lies in -0.25 to 0.25, plane 1 in 0.02 to 0.1, plane 2 in -1 to 1.
All inputs are finite; a program needn't handle non-finite values. No bound on the sum of `land_sea` on one device may be relied on, other than what follows from the above.
Results may differ from the reference program's by a relative error of at most 0.00002.
Values sent between devices are 32-bit elements; how exact they have to be, the bound alone decides.
No kernel may reach another device: no remote copies, remote signals or barrier semaphores. Data moves between devices by JAX's collectives and lax.ppermute only.
A program may use at most 64 MiB of HBM per device.

```python
import math
import jax
import jax.numpy as jnp

STEPS = 3
NX = 512
NY = 256
LEV = 6


def face_planes(key, inflow):
    subkeys = jax.random.split(key, 4)
    grid_shape = (LEV, NY, NX)
    velocity = jax.random.uniform(subkeys[0], grid_shape, jnp.float32, -0.25, 0.25)
    slopes = jax.random.uniform(subkeys[2], grid_shape, jnp.float32, -1.0, 1.0)
    if inflow > 0:
        row_index = jnp.arange(NY).reshape(1, NY, 1)
        top_speed = -0.1 - 0.15 * jax.random.uniform(subkeys[3], grid_shape, jnp.float32, 0.0, 1.0)
        velocity = jnp.where(row_index == NY - 1, top_speed, velocity)
    diffusivity = jnp.exp(jax.random.uniform(subkeys[1], grid_shape, jnp.float32, math.log(0.02), math.log(0.1)))
    return jnp.stack([velocity, diffusivity, slopes], 0)


def draw_tracers(key, part):
    key = jax.random.fold_in(key, 13)
    grid_shape = (2, LEV, NY, NX)
    values = jnp.clip(jax.random.normal(key, grid_shape, jnp.float32), -3.0, 3.0)
    row_index = jnp.arange(NY).reshape(1, 1, NY, 1)
    row_scale = jnp.where(row_index >= NY - 4, 4.0, 1.0).astype(jnp.float32)
    return values * row_scale


def draw_faces_east(key, part):
    key = jax.random.fold_in(key, 11)
    return face_planes(key, 0.0)


def draw_faces_north(key, part):
    key = jax.random.fold_in(key, 12)
    return face_planes(key, 1.0)


def plant(result, rng, smallest, largest):
    dims = result.shape
    index_at = [jax.random.randint(jax.random.fold_in(rng, axis), (), 0, dims[axis]) for axis in range(len(dims))]
    result = result.at[tuple(index_at)].set(smallest)
    longest = dims.index(max(dims))
    index_at[longest] = (index_at[longest] + 1) % dims[longest]
    return result.at[tuple(index_at)].set(largest)


def setup_inputs(seed: int = 0, part: int = 0) -> dict:
    splits = jax.random.split(jax.random.key(seed), 5)
    part_splits = jax.random.split(jax.random.fold_in(splits[4], part), 5)
    tracers = draw_tracers(jax.random.fold_in(jax.random.fold_in(splits[4], part), 71), part)
    land_sea = plant((jax.random.randint(splits[1], (LEV, NY, NX), 0, 4) < 3).astype(jnp.int32), jax.random.fold_in(splits[1], 1), 0, 1)
    faces_east = draw_faces_east(jax.random.fold_in(jax.random.fold_in(splits[4], part), 71), part)
    faces_north = draw_faces_north(jax.random.fold_in(jax.random.fold_in(splits[4], part), 71), part)
    return dict(tracers=tracers, land_sea=land_sea, faces_east=faces_east, faces_north=faces_north)


def face_flux(behind, forward, fields):
    velocity = fields[0]
    diffusivity = fields[1]
    slopes = fields[2]
    shared_wet = behind[2] * forward[2]
    upwind = 0.5 * (velocity + jnp.abs(velocity)) * behind[:2] + 0.5 * (velocity - jnp.abs(velocity)) * forward[:2]
    gradient = forward[:2] - behind[:2] - slopes * 0.25 * (behind[3:] + forward[3:])
    return shared_wet * (upwind - diffusivity * gradient)


def advance(current, wetness, faces_east, faces_north):
    wet_pad = jnp.pad(wetness, ((1, 1), (0, 0), (0, 0)))
    state_pad = jnp.pad(current, ((0, 0), (1, 1), (0, 0), (0, 0)))
    vertical = 0.5 * wet_pad[2:] * wetness * wet_pad[:-2] * (state_pad[:, 2:] - state_pad[:, :-2])
    planes = jnp.concatenate([current, wetness[None], vertical], 0)
    eastern = jnp.roll(planes, -1, axis=3)
    east_flux = face_flux(planes, eastern, faces_east)
    div_east = jnp.roll(east_flux, 1, axis=3) - east_flux
    top_row = planes[:, :, -1:, ::-1]
    northern = jnp.concatenate([planes[:, :, 1:], top_row], 2)
    north_flux = face_flux(planes, northern, faces_north)
    southern = jnp.concatenate([jnp.zeros_like(north_flux[:, :, :1]), north_flux[:, :, :-1]], 2)
    div_north = southern - north_flux
    return current + wetness * (div_east + div_north)


def reference(tracers, land_sea, faces_east, faces_north):
    wetness = land_sea.astype(jnp.float32)
    current = tracers
    for repeat in range(STEPS):
        current = advance(current, wetness, faces_east, faces_north)
    return current
```

```python
import jax
import jax.numpy as jnp
from jax import lax
from jax.experimental import pallas as pl
from jax.experimental.pallas import tpu as pltpu
from jax.sharding import PartitionSpec as P

STEPS = 3
S0, EV, S1, ED, ES, NV, ND, NS, WET = range(9)
R = 136
VMEM = pl.BlockSpec(memory_space=pltpu.VMEM)
PARAMS = pltpu.CompilerParams(vmem_limit_bytes=40 * 2**20)
f32 = jnp.float32


def iota(shape, dim):
    return lax.broadcasted_iota(jnp.int32, shape, dim)


def roll(x, shift, axis):
    shift %= x.shape[axis]
    return x if shift == 0 else pltpu.roll(x, shift, axis)


def position():
    lev = lax.axis_index("lev")
    lat = lax.axis_index("lat")
    odd = lax.rem(lat, 2) == 1
    last = lat == lax.axis_size("lat") - 1
    return lev, odd, last


def level(q, lev):
    return q + lev * (2 - 2 * q)


def raw(refs, n, kk, rows):
    tr, ls, fe, fn = refs
    if n == WET:
        return ls[kk, rows].astype(f32)
    if n in (S0, S1):
        return tr[n // 2, kk, rows]
    if n in (EV, ED, ES):
        return fe[(EV, ED, ES).index(n), kk, rows]
    return fn[n - NV, kk, rows]


def edges_kernel(tr, ls, fe, fn, strip_ref, east_ref, west_ref, lev_ref, a_ref, b_ref):
    refs = (tr, ls, fe, fn)
    lev, odd, last = position()
    lane = iota((8, 128), 1)
    m = lane % 10

    @pl.loop(0, 16)
    def _(t):
        rows = pl.ds(pl.multiple_of(t * 8, 8), 8)
        strips = []
        for i in range(3):
            strip = jnp.zeros((8, 128), f32)
            for n in range(4 * i, min(4 * i + 4, 9)):
                for q in range(3):
                    x = raw(refs, n, level(q, lev), rows)
                    if n in (S0, S1):
                        lev_ref[n // 2 * 3 + q, rows] = x
                    elif n == WET:
                        lev_ref[6 + q, rows] = x
                    elif q >= 1:
                        face = (EV, ED, ES, NV, ND, NS).index(n)
                        lev_ref[9 + face * 2 + q - 1, rows] = x
                    at = 30 * (n % 4) + 10 * q
                    strip = jnp.where((lane >= at) & (lane < at + 5), roll(x, at - 126, 1), strip)
                    strip = jnp.where((lane >= at + 5) & (lane < at + 10), roll(x, at + 5 - 125, 1), strip)
            strip_ref[i, rows] = strip
            strips.append(strip)
        s0, s1, s2 = strips
        east_ref[rows] = jnp.where(m < 3, roll(s0, -5, 1), jnp.where(m < 6, roll(s1, -2, 1), roll(s2, 1, 1)))
        west_ref[rows] = jnp.where(m < 3, roll(s0, -2, 1), jnp.where(m < 6, roll(s1, 1, 1), roll(s2, 4, 1)))

    sub = iota((8, 128), 0)

    def forms(p):
        if p >= 27:
            return (jnp.zeros((8, 128), f32),) * 3
        n, q = divmod(p, 3)
        kk = level(q, lev)
        top = raw(refs, n, kk, pl.ds(120, 8))
        bottom = raw(refs, n, kk, pl.ds(0, 8))
        flipped = jnp.take_along_axis(jnp.take_along_axis(top, 7 - sub, axis=0), 127 - lane, axis=1)
        if n in (EV, ED, ES):
            flipped = roll(flipped, -1, 1)
        if n in (EV, ES, NV, NS):
            flipped = -flipped
        return top, bottom, flipped

    for j in range(15):
        top, bottom, flipped = forms(j)
        top2, bottom2, flipped2 = forms(j + 15)
        as_south = jnp.where(sub >= 4, top, roll(top2, 4, 0))
        as_north = jnp.where(sub < 4, bottom, roll(bottom2, 4, 0))
        folded = jnp.where(sub < 4, flipped, roll(flipped2, 4, 0))
        a_ref[j] = jnp.where(odd, as_north, as_south)
        b_ref[j] = jnp.where(odd, jnp.where(last, folded, as_south), as_north)


def rows_kernel(strip, from_east, from_west, a_in, b_in, full_ref, a_ref, b_ref):
    lev, odd, last = position()
    lane = iota((128, 128), 1)
    m = lane % 10
    e, w = from_east[...], from_west[...]
    for i in range(3):
        full_ref[i] = jnp.where(
            (m >= 2) & (m < 5),
            roll(e, 2 - 3 * i, 1),
            jnp.where((m >= 5) & (m < 8), roll(w, 5 - 3 * i, 1), strip[i]),
        )
    lane = iota((8, 128), 1)
    sub = iota((8, 128), 0)
    m = lane % 10
    group = lane - m
    quarter = lane // 30
    turned = []
    for i in range(3):
        top, bottom = full_ref[i, pl.ds(120, 8)], full_ref[i, pl.ds(0, 8)]
        swapped = jnp.take_along_axis(top, 7 - sub, axis=0)
        turned.append(swapped)
        east_item = [(quarter == 1) | (quarter == 3), quarter == 0, quarter < 0][i]
        negative = [quarter == 1, (quarter == 0) | (quarter == 1) | (quarter == 3), quarter < 0][i]
        source = jnp.clip(group + jnp.where(east_item, 8, 9) - m, 0, 127)
        folded = jnp.take_along_axis(swapped, source, axis=1)
        folded = jnp.where(negative, -folded, folded)
        as_south, as_north, folded = roll(top, 4, 0), roll(bottom, 4, 0), roll(folded, 4, 0)
        j = 12 + i
        a_ref[j] = jnp.where(
            odd, jnp.where(sub < 4, a_in[j], as_north), jnp.where(sub >= 4, a_in[j], as_south)
        )
        b_south = jnp.where(sub >= 4, b_in[j], as_south)
        b_north = jnp.where(sub < 4, b_in[j], jnp.where(last, folded, as_north))
        b_ref[j] = jnp.where(jnp.logical_and(odd, jnp.logical_not(last)), b_south, b_north)
    for j in range(12):
        a_ref[j] = a_in[j]
        if j not in (3, 4, 5, 9, 10, 11):
            b_ref[j] = b_in[j]
    for n in (EV, ED, ES):
        for q in range(3):
            j = 3 * n + q
            at = 30 * (n % 4) + 10 * q + 7
            x = roll(turned[n // 4], 127 - at, 1)
            x = x if n == ED else -x
            old = b_in[j] if j < 12 else b_ref[j]
            b_ref[j] = jnp.where((lane == 127) & (sub < 4) & last, x, old)


def coefficients(v, d, slope, wet):
    return (
        wet * (jnp.maximum(v, 0.0) + d),
        wet * (jnp.minimum(v, 0.0) - d),
        wet * (d * 0.25 * slope),
    )


def steps_kernel(
    tr, ls, fe, fn, lev_in, strip_o, strip_p, a_o, b_o, a_p, b_p,
    out, S, W, K, K2, F, SS, SK, SK2, G,
):
    lev, odd, last = position()
    refs = (tr, ls, fe, fn)
    lane = iota((8, 128), 1)
    sub = iota((8, 128), 0)
    zero = jnp.zeros((8, 128), f32)
    tiles = [pl.ds(8 * t, 8) for t in range(17)]

    def halo(p, partner):
        a, b = (a_p, b_p) if partner else (a_o, b_o)
        x, y = a[p % 15], b[p % 15]
        north, south = jnp.where(odd, y, x), jnp.where(odd, x, y)
        if p >= 15:
            north, south = roll(north, 4, 0), roll(south, 4, 0)
        return north, jnp.where(sub >= 5, south, 0.0)

    def halo_tile(n, q, partner):
        north, south = halo(3 * n + q, partner)
        if n in (NV, ND, NS):
            return jnp.where(sub < 2, jnp.where(last, roll(north, -1, 0), north), south), north
        return jnp.where(sub < 3, north, south), north

    half = jnp.where(lev == 0, 0.5, -0.5)

    for buffer in range(2):
        for c in range(2):
            S[buffer, c, 0] = jnp.zeros((R, 128), f32)
    W[0] = jnp.zeros((R, 128), f32)
    for q in range(3):
        kk = level(q, lev)
        for c in range(2):
            S[0, c, q + 1, pl.ds(0, 128)] = tr[c, kk]
            S[0, c, q + 1, tiles[16]] = halo_tile((S0, S1)[c], q, False)[0]
            S[0, c, 6 - q, pl.ds(0, 128)] = lev_in[3 * c + q]
            S[0, c, 6 - q, tiles[16]] = halo_tile((S0, S1)[c], q, True)[0]
        W[q + 1, pl.ds(0, 128)] = ls[kk].astype(f32)
        W[q + 1, tiles[16]] = halo_tile(WET, q, False)[0]
        W[6 - q, pl.ds(0, 128)] = lev_in[6 + q]
        W[6 - q, tiles[16]] = halo_tile(WET, q, True)[0]

    m = lane % 10
    group = lane // 10
    q_here = group % 6
    mine = q_here < 3
    used = lane < 120
    own_at = 10 * q_here + m
    partner_at = 10 * (5 - q_here) + m
    strip_south = [None] * 3

    for t in range(17):
        own, other = [], []
        for i in range(3):
            if t < 16:
                own.append(strip_o[i, tiles[t]])
                other.append(strip_p[i, tiles[t]])
            else:
                own.append(halo(27 + i, False))
                other.append(halo(27 + i, True))
        for n in range(9):
            if n == S1:
                continue
            if n == S0:
                index = jnp.where(mine, own_at, partner_at) + jnp.where(group >= 6, 60, 0)
            else:
                index = 30 * (n % 4) + jnp.where(mine, own_at, partner_at)
            index = jnp.clip(index, 0, 127)

            def spread(x, y):
                x = jnp.take_along_axis(x, index, axis=1)
                y = jnp.take_along_axis(y, index, axis=1)
                return jnp.where(used, jnp.where(mine, x, y), 0.0)

            if t < 16:
                F[n, tiles[t]] = spread(own[n // 4], other[n // 4])
            else:
                north = spread(own[n // 4][0], other[n // 4][0])
                south = spread(own[n // 4][1], other[n // 4][1])
                if n in (NV, ND, NS):
                    strip_south[n - NV] = north
                    F[n, tiles[t]] = jnp.where(
                        sub < 2, jnp.where(last, roll(north, -1, 0), north), south
                    )
                else:
                    F[n, tiles[t]] = jnp.where(sub < 3, north, south)

    def up(values, t):
        return jnp.where(sub == 7, roll(values[(t + 1) % 17], -1, 0), roll(values[t], -1, 0))

    def down(values, t):
        return jnp.where(sub == 0, roll(values[(t - 1) % 17], 1, 0), roll(values[t], 1, 0))

    def north_coefficients(v, d, s, wet, v2, d2, s2, put, put2):
        pairs = {}
        for t in [16] + list(range(17)):
            if t in pairs and t == 16:
                a, b, c = pairs[16]
            else:
                wet_t = wet(t) * up([wet(i) if i in (t, (t + 1) % 17) else None for i in range(17)], t)
                a, b, c = coefficients(v(t), d(t), s(t), wet_t)
                pairs[t] = a, b, c
                if t == 15:
                    x, y, z = coefficients(roll(v2, -1, 0), roll(d2, -1, 0), roll(s2, -1, 0), wet_t)
                    far = jnp.logical_and(last, sub == 7)
                    a2, b2, c2 = jnp.where(far, x, a), jnp.where(far, y, b), jnp.where(far, z, c)
                    put2(0, a2)
                    put2(1, c2)
            if (t - 1) % 17 in pairs:
                _, b0, c0 = pairs[(t - 1) % 17]
                put(t, 4, a)
                put(t, 5, c)
                put(t, 6, jnp.where(sub == 0, roll(b0, 1, 0), roll(b, 1, 0)))
                put(t, 7, jnp.where(sub == 0, roll(c0, 1, 0), roll(c, 1, 0)))
                if t == 16:
                    put2(2, jnp.where(sub == 0, roll(b2, 1, 0), roll(b, 1, 0)))
                    put2(3, jnp.where(sub == 0, roll(c2, 1, 0), roll(c, 1, 0)))

    for t in range(17):
        wet = F[WET, tiles[t]]
        a, b, c = coefficients(F[EV, tiles[t]], F[ED, tiles[t]], F[ES, tiles[t]], wet * roll(wet, -1, 1))
        SK[0, tiles[t]] = a
        SK[1, tiles[t]] = c
        SK[2, tiles[t]] = roll(b, 1, 1)
        SK[3, tiles[t]] = roll(c, 1, 1)
        outside = (q_here == 0) | (q_here == 5)
        around = roll(wet, -10, 1) * roll(wet, 10, 1)
        SK[8, tiles[t]] = jnp.where(outside, 0.0, half * wet * around)
        SS[0, tiles[t]] = F[S0, tiles[t]]

    def put_strip(t, at, x):
        SK[at, tiles[t]] = x

    def put_strip2(at, x):
        SK2[at] = x

    north_coefficients(
        lambda t: F[NV, tiles[t]], lambda t: F[ND, tiles[t]], lambda t: F[NS, tiles[t]],
        lambda t: F[WET, tiles[t]], *strip_south, put_strip, put_strip2,
    )

    for q in range(5):
        partner = q >= 3
        qq = 5 - q if partner else q
        kk = level(q, lev)

        def field(n, t):
            if t == 16:
                return halo_tile(n, qq, partner)[0]
            if partner:
                face = (EV, ED, ES, NV, ND, NS).index(n)
                return lev_in[9 + face * 2 + qq - 1, tiles[t]]
            return raw(refs, n, kk, tiles[t])

        for t in range(17):
            wet = W[q + 1, tiles[t]]
            beyond = roll(F[WET, tiles[t]], 127 - (10 * q + 2), 1)
            ahead = jnp.where(lane == 127, beyond, roll(wet, -1, 1))
            a, b, c = coefficients(field(EV, t), field(ED, t), field(ES, t), wet * ahead)
            K[q, 0, tiles[t]] = a
            K[q, 1, tiles[t]] = c
            K[q, 2, tiles[t]] = jnp.where(lane == 0, roll(SK[2, tiles[t]], -(10 * q + 8), 1), roll(b, 1, 1))
            K[q, 3, tiles[t]] = jnp.where(lane == 0, roll(SK[3, tiles[t]], -(10 * q + 8), 1), roll(c, 1, 1))
            K[q, 8, tiles[t]] = half * W[q, tiles[t]] * wet * W[q + 2, tiles[t]]

        def put(t, at, x):
            K[q, at, tiles[t]] = x

        def put2(at, x):
            K2[q, at] = x

        north_coefficients(
            lambda t: field(NV, t), lambda t: field(ND, t), lambda t: field(NS, t),
            lambda t: W[q + 1, tiles[t]],
            halo_tile(NV, qq, partner)[1], halo_tile(ND, qq, partner)[1], halo_tile(NS, qq, partner)[1],
            put, put2,
        )

    def sweep(coef, coef2, state, vertical, sides, store, final):
        held = {}

        def terms(t):
            s, u = state(t), vertical(t)
            up_face = coef(t, 4) * s + coef(t, 5) * u
            down_face = coef(t, 6) * s + coef(t, 7) * u
            far, near = up_face, down_face
            if t == 15:
                far = coef2(0) * s + coef2(1) * u
            if t == 16:
                near = coef2(2) * s + coef2(3) * u
            part = None
            if not (final and t == 16):
                east, west = coef(t, 0) * s + coef(t, 1) * u, coef(t, 2) * s + coef(t, 3) * u
                part = s + sides(t, east, west) + (near - up_face)
            held[t] = part, roll(up_face, 1, 0), roll(far, 1, 0), roll(down_face, -1, 0)

        terms(16)
        terms(0)
        for t in range(17):
            if t == 16 and final:
                break
            if t < 15:
                terms(t + 1)
            part, x, _, y = held[t]
            before = held[(t - 1) % 17]
            after = held[(t + 1) % 17]
            x = jnp.where(sub == 0, before[2], x)
            y = jnp.where(sub == 7, after[3], y)
            store(t, part + (x - y))

    for step in range(STEPS):
        now, later = step % 2, 1 - step % 2
        final = step == STEPS - 1

        def strip_vertical(t):
            s = SS[now, tiles[t]]
            return SK[8, tiles[t]] * (roll(s, -10, 1) - roll(s, 10, 1))

        def strip_sides(t, east, west):
            G[tiles[t]] = jnp.where(m == 3, roll(east, -4, 1), west)
            return roll(east, 1, 1) - east + west - roll(west, -1, 1)

        def strip_store(t, x):
            SS[later, tiles[t]] = x

        sweep(
            lambda t, i: SK[i, tiles[t]], lambda i: SK2[i],
            lambda t: SS[now, tiles[t]], strip_vertical, strip_sides, strip_store, final,
        )

        @pl.loop(0, 5 - step)
        def _(q):
            for c in range(2):
                def vertical(t):
                    return K[q, 8, tiles[t]] * (S[now, c, q + 2, tiles[t]] - S[now, c, q, tiles[t]])

                def sides(t, east, west):
                    edge = pltpu.roll(G[tiles[t]], 125 + 128 - 10 * (6 * c + q), 1)
                    x = jnp.where(lane == 0, edge, roll(east, 1, 1))
                    y = jnp.where(lane == 127, edge, roll(west, -1, 1))
                    return (x - east) + (west - y)

                def store(t, x):
                    if final:
                        out[c, level(q, lev), tiles[t]] = x
                    else:
                        S[later, c, q + 1, tiles[t]] = x

                sweep(
                    lambda t, i: K[q, i, tiles[t]], lambda i: K2[q, i],
                    lambda t: S[now, c, q + 1, tiles[t]], vertical, sides, store, final,
                )


def call(kernel, shapes, scratch=()):
    return pl.pallas_call(
        kernel,
        out_shape=[jax.ShapeDtypeStruct(s, f32) for s in shapes],
        out_specs=[VMEM] * len(shapes),
        scratch_shapes=[pltpu.VMEM(s, f32) for s in scratch],
        compiler_params=PARAMS,
    )


def local(tracers, land_sea, faces_east, faces_north):
    lons, lats = lax.axis_size("lon"), lax.axis_size("lat")
    swap = [(0, 1), (1, 0)]

    strip, to_east, to_west, levels, rows_a, rows_b = call(
        edges_kernel,
        [(3, 128, 128), (128, 128), (128, 128), (21, 128, 128), (15, 8, 128), (15, 8, 128)],
    )(tracers, land_sea, faces_east, faces_north)
    lev_in = lax.ppermute(levels, "lev", swap)
    from_west = lax.ppermute(to_east, "lon", [(i, (i + 1) % lons) for i in range(lons)])
    from_east = lax.ppermute(to_west, "lon", [((i + 1) % lons, i) for i in range(lons)])
    full, rows_a, rows_b = call(rows_kernel, [(3, 128, 128), (15, 8, 128), (15, 8, 128)])(
        strip, from_east, from_west, rows_a, rows_b
    )

    def at(lon, lat):
        return lon * lats + lat

    route_a, route_b = [], []
    for lon in range(lons):
        for lat in range(lats):
            other = lat + 1 if lat % 2 == 0 else lat - 1
            route_a.append((at(lon, lat), at(lon, other)))
            if lat == lats - 1:
                route_b.append((at(lon, lat), at(lons - 1 - lon, lat)))
            elif lat > 0:
                other = lat - 1 if lat % 2 == 0 else lat + 1
                route_b.append((at(lon, lat), at(lon, other)))
    got_a = lax.ppermute(rows_a, ("lon", "lat"), route_a)
    got_b = lax.ppermute(rows_b, ("lon", "lat"), route_b)
    full_p = lax.ppermute(full, "lev", swap)
    got_a_p = lax.ppermute(got_a, "lev", swap)
    got_b_p = lax.ppermute(got_b, "lev", swap)

    (out,) = call(
        steps_kernel,
        [(2, 3, 128, 128)],
        [
            (2, 2, 7, R, 128), (7, R, 128), (5, 9, R, 128), (5, 4, 8, 128),
            (9, R, 128), (2, R, 128), (9, R, 128), (4, 8, 128), (R, 128),
        ],
    )(tracers, land_sea, faces_east, faces_north, lev_in, full, full_p, got_a, got_b, got_a_p, got_b_p)
    return out


def solution(mesh):
    return jax.shard_map(
        local,
        mesh=mesh,
        in_specs=(
            P("members", "lev", "lat", "lon"),
            P("lev", "lat", "lon"),
            P("members", "lev", "lat", "lon"),
            P("members", "lev", "lat", "lon"),
        ),
        out_specs=P("members", "lev", "lat", "lon"),
        check_vma=False,
    )
```

```python
import jax
import jax.numpy as jnp
from jax import lax
from jax.experimental import pallas as pl
from jax.experimental.pallas import tpu as pltpu
from jax.sharding import PartitionSpec as P

STEPS = 3
S0, EV, S1, ED, ES, NV, ND, NS, WET = range(9)
R = 136
VMEM = pl.BlockSpec(memory_space=pltpu.VMEM)
PARAMS = pltpu.CompilerParams(vmem_limit_bytes=40 * 2**20)
f32 = jnp.float32


def iota(shape, dim):
    return lax.broadcasted_iota(jnp.int32, shape, dim)


def roll(x, shift, axis):
    shift %= x.shape[axis]
    return x if shift == 0 else pltpu.roll(x, shift, axis)


def position():
    lev = lax.axis_index("lev")
    lat = lax.axis_index("lat")
    odd = lax.rem(lat, 2) == 1
    last = lat == lax.axis_size("lat") - 1
    return lev, odd, last


def level(q, lev):
    return q + lev * (2 - 2 * q)


def raw(refs, n, kk, rows):
    tr, ls, fe, fn = refs
    if n == WET:
        return ls[kk, rows].astype(f32)
    if n in (S0, S1):
        return tr[n // 2, kk, rows]
    if n in (EV, ED, ES):
        return fe[(EV, ED, ES).index(n), kk, rows]
    return fn[n - NV, kk, rows]


def edges_kernel(tr, ls, fe, fn, tr_v, ls_v, fe_v, fn_v, edge_ref, east_ref, west_ref, sem):
    lev, _, _ = position()
    lane = iota((8, 128), 1)
    m = lane % 10
    sources, targets = (tr, ls, fe, fn), (tr_v, ls_v, fe_v, fn_v)
    copies = []
    for i in range(3):
        copies.append([])
        for n in range(4 * i, min(4 * i + 4, 9)):
            if n == WET:
                which, lead = 1, ()
            elif n in (S0, S1):
                which, lead = 0, (n // 2,)
            elif n in (EV, ED, ES):
                which, lead = 2, ((EV, ED, ES).index(n),)
            else:
                which, lead = 3, (n - NV,)
            source, target = sources[which], targets[which]
            if lead:
                source, target = source.at[lead[0]], target.at[lead[0]]
            copy = pltpu.make_async_copy(source, target, sem.at[n])
            copy.start()
            copies[i].append(copy)
    for i in range(3):
        for copy in copies[i]:
            copy.wait()
        for t in range(16):
            rows = pl.ds(8 * t, 8)
            packed = jnp.zeros((8, 128), f32)
            for n in range(4 * i, min(4 * i + 4, 9)):
                for q in range(3):
                    x = raw(targets, n, level(q, lev), rows)
                    at = 30 * (n % 4) + 10 * q + 3 * i
                    packed = jnp.where((lane >= at) & (lane < at + 6), roll(x, at - 125, 1), packed)
            edge_ref[i, rows] = packed
    for t in range(16):
        rows = pl.ds(8 * t, 8)
        a, b, c = edge_ref[0, rows], edge_ref[1, rows], edge_ref[2, rows]
        east_ref[rows] = jnp.where(m < 3, a, jnp.where(m < 6, b, c))
        west_ref[rows] = jnp.where((m >= 3) & (m < 6), a, jnp.where((m >= 6) & (m < 9), b, c))


def planes_kernel(tr, ls, fe, fn, edge, strip_ref, lev_ref, a_ref, b_ref):
    refs = (tr, ls, fe, fn)
    lev, odd, last = position()
    lane = iota((8, 128), 1)
    m = lane % 10
    for i in range(3):
        for t in range(16):
            rows = pl.ds(8 * t, 8)
            x = edge[i, rows]
            strip_ref[i, rows] = jnp.where(m < 5, roll(x, -1 - 3 * i, 1), roll(x, 5 - 3 * i, 1))
    for q in range(3):
        kk = level(q, lev)
        for c in range(2):
            lev_ref[3 * c + q] = tr[c, kk]
        lev_ref[6 + q] = ls[kk].astype(f32)
        if q >= 1:
            for face in range(3):
                lev_ref[9 + face * 2 + q - 1] = fe[face, kk]
                lev_ref[15 + face * 2 + q - 1] = fn[face, kk]

    sub = iota((8, 128), 0)

    def ends(p):
        if p >= 27:
            return (jnp.zeros((8, 128), f32),) * 2
        n, q = divmod(p, 3)
        kk = level(q, lev)
        return raw(refs, n, kk, pl.ds(120, 8)), raw(refs, n, kk, pl.ds(0, 8))

    for j in range(15):
        n, n2 = j // 3, (j + 15) // 3
        top, bottom = ends(j)
        top2, bottom2 = ends(j + 15)
        as_south = jnp.where(sub >= 4, top, roll(top2, 4, 0))
        as_north = jnp.where(sub < 4, bottom, roll(bottom2, 4, 0))
        folded = jnp.take_along_axis(jnp.take_along_axis(as_south, 7 - sub, axis=0), 127 - lane, axis=1)
        if n in (EV, ED, ES):
            folded = jnp.where(sub < 4, roll(folded, -1, 1), folded)
        if n in (EV, ES):
            folded = jnp.where(sub < 4, -folded, folded)
        if n2 in (NV, NS):
            folded = jnp.where(sub >= 4, -folded, folded)
        a_ref[j] = jnp.where(odd, as_north, as_south)
        b_ref[j] = jnp.where(odd, jnp.where(last, folded, as_south), as_north)


def rows_kernel(strip, from_east, from_west, a_in, b_in, full_ref, a_ref, b_ref):
    lev, odd, last = position()
    lane = iota((128, 128), 1)
    m = lane % 10
    e, w = from_east[...], from_west[...]
    for i in range(3):
        full_ref[i] = jnp.where(
            (m >= 2) & (m < 5),
            roll(e, -1 - 3 * i, 1),
            jnp.where((m >= 5) & (m < 8), roll(w, 5 - 3 * i, 1), strip[i]),
        )
    lane = iota((8, 128), 1)
    sub = iota((8, 128), 0)
    m = lane % 10
    group = lane - m
    quarter = lane // 30
    turned = []
    for i in range(3):
        top, bottom = full_ref[i, pl.ds(120, 8)], full_ref[i, pl.ds(0, 8)]
        swapped = jnp.take_along_axis(top, 7 - sub, axis=0)
        turned.append(swapped)
        east_item = [(quarter == 1) | (quarter == 3), quarter == 0, quarter < 0][i]
        negative = [quarter == 1, (quarter == 0) | (quarter == 1) | (quarter == 3), quarter < 0][i]
        source = jnp.clip(group + jnp.where(east_item, 8, 9) - m, 0, 127)
        folded = jnp.take_along_axis(swapped, source, axis=1)
        folded = jnp.where(negative, -folded, folded)
        as_south, as_north, folded = roll(top, 4, 0), roll(bottom, 4, 0), roll(folded, 4, 0)
        j = 12 + i
        a_ref[j] = jnp.where(
            odd, jnp.where(sub < 4, a_in[j], as_north), jnp.where(sub >= 4, a_in[j], as_south)
        )
        b_south = jnp.where(sub >= 4, b_in[j], as_south)
        b_north = jnp.where(sub < 4, b_in[j], jnp.where(last, folded, as_north))
        b_ref[j] = jnp.where(jnp.logical_and(odd, jnp.logical_not(last)), b_south, b_north)
    for j in range(12):
        a_ref[j] = a_in[j]
        if j not in (3, 4, 5, 9, 10, 11):
            b_ref[j] = b_in[j]
    for n in (EV, ED, ES):
        for q in range(3):
            j = 3 * n + q
            at = 30 * (n % 4) + 10 * q + 7
            x = roll(turned[n // 4], 127 - at, 1)
            x = x if n == ED else -x
            old = b_in[j] if j < 12 else b_ref[j]
            b_ref[j] = jnp.where((lane == 127) & (sub < 4) & last, x, old)


def coefficients(v, d, slope, wet):
    return (
        wet * (jnp.maximum(v, 0.0) + d),
        wet * (jnp.minimum(v, 0.0) - d),
        wet * (d * 0.25 * slope),
    )


def steps_kernel(
    tr, ls, fe, fn, lev_in, strip_o, strip_p, a_o, b_o, a_p, b_p,
    out, SA, SB, W, K, K2, F, SS0, SS1, SK, SK2, G, U, D,
):
    lev, odd, last = position()
    refs = (tr, ls, fe, fn)
    lane = iota((8, 128), 1)
    sub = iota((8, 128), 0)
    zero = jnp.zeros((8, 128), f32)
    tiles = [pl.ds(8 * t, 8) for t in range(17)]

    def halo(p, partner):
        a, b = (a_p, b_p) if partner else (a_o, b_o)
        x, y = a[p % 15], b[p % 15]
        north, south = jnp.where(odd, y, x), jnp.where(odd, x, y)
        if p >= 15:
            north, south = roll(north, 4, 0), roll(south, 4, 0)
        return north, jnp.where(sub >= 5, south, 0.0)

    def halo_tile(n, q, partner):
        north, south = halo(3 * n + q, partner)
        if n in (NV, ND, NS):
            return jnp.where(sub < 2, jnp.where(last, roll(north, -1, 0), north), south), north
        return jnp.where(sub < 3, north, south), north

    half = jnp.where(lev == 0, 0.5, -0.5)

    for buffer in range(2):
        for c in range(2):
            (SA, SB)[buffer][c, 0] = jnp.zeros((R, 128), f32)
    W[0] = jnp.zeros((R, 128), f32)
    for q in range(3):
        kk = level(q, lev)
        for c in range(2):
            SA[c, q + 1, pl.ds(0, 128)] = tr[c, kk]
            SA[c, q + 1, tiles[16]] = halo_tile((S0, S1)[c], q, False)[0]
            SA[c, 6 - q, pl.ds(0, 128)] = lev_in[3 * c + q]
            SA[c, 6 - q, tiles[16]] = halo_tile((S0, S1)[c], q, True)[0]
        W[q + 1, pl.ds(0, 128)] = ls[kk].astype(f32)
        W[q + 1, tiles[16]] = halo_tile(WET, q, False)[0]
        W[6 - q, pl.ds(0, 128)] = lev_in[6 + q]
        W[6 - q, tiles[16]] = halo_tile(WET, q, True)[0]

    m = lane % 10
    group = lane // 10
    q_here = group % 6
    mine = q_here < 3
    used = lane < 120
    own_at = 10 * q_here + m
    partner_at = 10 * (5 - q_here) + m
    strip_south = [None] * 3

    for t in range(17):
        own, other = [], []
        for i in range(3):
            if t < 16:
                own.append(strip_o[i, tiles[t]])
                other.append(strip_p[i, tiles[t]])
            else:
                own.append(halo(27 + i, False))
                other.append(halo(27 + i, True))
        for n in range(9):
            if n == S1:
                continue
            if n == S0:
                index = jnp.where(mine, own_at, partner_at) + jnp.where(group >= 6, 60, 0)
            else:
                index = 30 * (n % 4) + jnp.where(mine, own_at, partner_at)
            index = jnp.clip(index, 0, 127)

            def spread(x, y):
                x = jnp.take_along_axis(x, index, axis=1)
                y = jnp.take_along_axis(y, index, axis=1)
                return jnp.where(used, jnp.where(mine, x, y), 0.0)

            if t < 16:
                F[n, tiles[t]] = spread(own[n // 4], other[n // 4])
            else:
                north = spread(own[n // 4][0], other[n // 4][0])
                south = spread(own[n // 4][1], other[n // 4][1])
                if n in (NV, ND, NS):
                    strip_south[n - NV] = north
                    F[n, tiles[t]] = jnp.where(
                        sub < 2, jnp.where(last, roll(north, -1, 0), north), south
                    )
                else:
                    F[n, tiles[t]] = jnp.where(sub < 3, north, south)

    def up(values, t):
        return jnp.where(sub == 7, roll(values[(t + 1) % 17], -1, 0), roll(values[t], -1, 0))

    def down(values, t):
        return jnp.where(sub == 0, roll(values[(t - 1) % 17], 1, 0), roll(values[t], 1, 0))

    def north_coefficients(v, d, s, wet, v2, d2, s2, put, put2):
        pairs = {}
        for t in [16] + list(range(17)):
            if t in pairs and t == 16:
                a, b, c = pairs[16]
            else:
                wet_t = wet(t) * up([wet(i) if i in (t, (t + 1) % 17) else None for i in range(17)], t)
                a, b, c = coefficients(v(t), d(t), s(t), wet_t)
                pairs[t] = a, b, c
                if t == 15:
                    x, y, z = coefficients(roll(v2, -1, 0), roll(d2, -1, 0), roll(s2, -1, 0), wet_t)
                    far = jnp.logical_and(last, sub == 7)
                    a2, b2, c2 = jnp.where(far, x, a), jnp.where(far, y, b), jnp.where(far, z, c)
                    put2(0, a2)
                    put2(1, c2)
            if (t - 1) % 17 in pairs:
                _, b0, c0 = pairs[(t - 1) % 17]
                put(t, 4, a)
                put(t, 5, c)
                put(t, 6, jnp.where(sub == 0, roll(b0, 1, 0), roll(b, 1, 0)))
                put(t, 7, jnp.where(sub == 0, roll(c0, 1, 0), roll(c, 1, 0)))
                if t == 16:
                    put2(2, jnp.where(sub == 0, roll(b2, 1, 0), roll(b, 1, 0)))
                    put2(3, jnp.where(sub == 0, roll(c2, 1, 0), roll(c, 1, 0)))

    for t in range(17):
        wet = F[WET, tiles[t]]
        a, b, c = coefficients(F[EV, tiles[t]], F[ED, tiles[t]], F[ES, tiles[t]], wet * roll(wet, -1, 1))
        SK[0, tiles[t]] = a
        SK[1, tiles[t]] = c
        SK[2, tiles[t]] = roll(b, 1, 1)
        SK[3, tiles[t]] = roll(c, 1, 1)
        outside = (q_here == 0) | (q_here == 5)
        around = roll(wet, -10, 1) * roll(wet, 10, 1)
        SK[8, tiles[t]] = jnp.where(outside, 0.0, half * wet * around)
        SS0[tiles[t]] = F[S0, tiles[t]]

    def put_strip(t, at, x):
        SK[at, tiles[t]] = x

    def put_strip2(at, x):
        SK2[at] = x

    north_coefficients(
        lambda t: F[NV, tiles[t]], lambda t: F[ND, tiles[t]], lambda t: F[NS, tiles[t]],
        lambda t: F[WET, tiles[t]], *strip_south, put_strip, put_strip2,
    )

    for q in range(5):
        partner = q >= 3
        qq = 5 - q if partner else q
        kk = level(q, lev)

        def field(n, t):
            if t == 16:
                return halo_tile(n, qq, partner)[0]
            if partner:
                face = (EV, ED, ES, NV, ND, NS).index(n)
                return lev_in[9 + face * 2 + qq - 1, tiles[t]]
            return raw(refs, n, kk, tiles[t])

        for t in range(17):
            wet = W[q + 1, tiles[t]]
            beyond = roll(F[WET, tiles[t]], 127 - (10 * q + 2), 1)
            D[0, 0, tiles[t]] = wet * jnp.where(lane == 127, beyond, roll(wet, -1, 1))
            K[q, 8, tiles[t]] = half * W[q, tiles[t]] * wet * W[q + 2, tiles[t]]
            D[0, 1, tiles[t]] = roll(SK[2, tiles[t]], -(10 * q + 8), 1)
            D[0, 2, tiles[t]] = roll(SK[3, tiles[t]], -(10 * q + 8), 1)
        for t in range(17):
            a, b, c = coefficients(field(EV, t), field(ED, t), field(ES, t), D[0, 0, tiles[t]])
            K[q, 0, tiles[t]] = a
            K[q, 1, tiles[t]] = c
            D[1, 1, tiles[t]] = roll(b, 1, 1)
            D[1, 2, tiles[t]] = roll(c, 1, 1)
        for t in range(17):
            K[q, 2, tiles[t]] = jnp.where(lane == 0, D[0, 1, tiles[t]], D[1, 1, tiles[t]])
            K[q, 3, tiles[t]] = jnp.where(lane == 0, D[0, 2, tiles[t]], D[1, 2, tiles[t]])

        def put(t, at, x):
            K[q, at, tiles[t]] = x

        def put2(at, x):
            K2[q, at] = x

        north_coefficients(
            lambda t: field(NV, t), lambda t: field(ND, t), lambda t: field(NS, t),
            lambda t: W[q + 1, tiles[t]],
            halo_tile(NV, qq, partner)[1], halo_tile(ND, qq, partner)[1], halo_tile(NS, qq, partner)[1],
            put, put2,
        )

    def terms(coef, coef2, state, vertical, final, push):
        held = {}

        def make(t):
            s, u = state(t), vertical(t)
            up_face = coef(t, 4) * s + coef(t, 5) * u
            down_face = coef(t, 6) * s + coef(t, 7) * u
            far, near = up_face, down_face
            if t == 15:
                far = coef2(0) * s + coef2(1) * u
            if t == 16:
                near = coef2(2) * s + coef2(3) * u
            part = None
            if not (final and t == 16):
                east, west = coef(t, 0) * s + coef(t, 1) * u, coef(t, 2) * s + coef(t, 3) * u
                push(t, east, west)
                part = s + (west - east) + (near - up_face)
            held[t] = part, roll(up_face, 1, 0), roll(far, 1, 0), roll(down_face, -1, 0)

        make(16)
        make(0)
        for t in range(17):
            if t == 16 and final:
                break
            if t < 15:
                make(t + 1)
            part, x, _, y = held[t]
            x = jnp.where(sub == 0, held[(t - 1) % 17][2], x)
            y = jnp.where(sub == 7, held[(t + 1) % 17][3], y)
            yield t, part + (x - y)

    for step in range(STEPS):
        (now, later), (snow, slater) = ((SA, SB), (SS0, SS1)) if step % 2 == 0 else ((SB, SA), (SS1, SS0))
        final = step == STEPS - 1

        for t in range(17):
            s = snow[tiles[t]]
            U[tiles[t]] = SK[8, tiles[t]] * (roll(s, -10, 1) - roll(s, 10, 1))

        def strip_push(t, east, west):
            G[tiles[t]] = jnp.where(m == 3, roll(east, -4, 1), west)
            D[0, 0, tiles[t]] = roll(east, 1, 1)
            D[0, 1, tiles[t]] = roll(west, -1, 1)

        for t, part in terms(
            lambda t, i: SK[i, tiles[t]], lambda i: SK2[i],
            lambda t: snow[tiles[t]], lambda t: U[tiles[t]], final, strip_push,
        ):
            if not final:
                D[0, 2, tiles[t]] = part
        if not final:
            for t in range(17):
                slater[tiles[t]] = D[0, 2, tiles[t]] + (D[0, 0, tiles[t]] - D[0, 1, tiles[t]])

        @pl.loop(0, 5 - step)
        def _(q):
            for c in range(2):
                def push(t, east, west):
                    D[c, 0, tiles[t]] = roll(east, 1, 1)
                    D[c, 1, tiles[t]] = roll(west, -1, 1)
                    D[c, 3, tiles[t]] = pltpu.roll(G[tiles[t]], 125 + 128 - 10 * (6 * c + q), 1)

                def vertical(t):
                    return K[q, 8, tiles[t]] * (now[c, q + 2, tiles[t]] - now[c, q, tiles[t]])

                for t, part in terms(
                    lambda t, i: K[q, i, tiles[t]], lambda i: K2[q, i],
                    lambda t: now[c, q + 1, tiles[t]], vertical, final, push,
                ):
                    D[c, 2, tiles[t]] = part
            for c in range(2):
                for t in range(16 if final else 17):
                    edge = D[c, 3, tiles[t]]
                    x = jnp.where(lane == 0, edge, D[c, 0, tiles[t]])
                    y = jnp.where(lane == 127, edge, D[c, 1, tiles[t]])
                    x = D[c, 2, tiles[t]] + (x - y)
                    if final:
                        out[c, level(q, lev), tiles[t]] = x
                    else:
                        later[c, q + 1, tiles[t]] = x


def call(kernel, shapes, scratch=(), types=(), in_specs=None, cost=None):
    types = list(types) + [f32] * (len(shapes) - len(types))
    return pl.pallas_call(
        kernel,
        out_shape=[jax.ShapeDtypeStruct(s, d) for s, d in zip(shapes, types)],
        **({} if in_specs is None else dict(in_specs=in_specs)),
        out_specs=[VMEM] * len(shapes),
        scratch_shapes=[pltpu.VMEM(s, f32) if isinstance(s, tuple) else s for s in scratch],
        compiler_params=PARAMS,
        cost_estimate=cost and pl.CostEstimate(flops=cost, bytes_accessed=cost, transcendentals=0),
    )


def local(tracers, land_sea, faces_east, faces_north):
    lons, lats = lax.axis_size("lon"), lax.axis_size("lat")
    swap = [(0, 1), (1, 0)]

    *blocks, edge, to_east, to_west = call(
        edges_kernel,
        [x.shape for x in (tracers, land_sea, faces_east, faces_north)] + [(3, 128, 128), (128, 128), (128, 128)],
        [pltpu.SemaphoreType.DMA((9,))],
        types=[x.dtype for x in (tracers, land_sea, faces_east, faces_north)],
        in_specs=[pl.BlockSpec(memory_space=pltpu.HBM)] * 4,
    )(*[pltpu.with_memory_space_constraint(x, pltpu.HBM) for x in (tracers, land_sea, faces_east, faces_north)])
    from_west = lax.ppermute(to_east, "lon", [(i, (i + 1) % lons) for i in range(lons)])
    from_east = lax.ppermute(to_west, "lon", [((i + 1) % lons, i) for i in range(lons)])
    strip, levels, rows_a, rows_b = call(
        planes_kernel, [(3, 128, 128), (21, 128, 128), (15, 8, 128), (15, 8, 128)], cost=20_000_000
    )(*blocks, edge)
    lev_in = lax.ppermute(levels, "lev", swap)
    full, rows_a, rows_b = call(rows_kernel, [(3, 128, 128), (15, 8, 128), (15, 8, 128)])(
        strip, from_east, from_west, rows_a, rows_b
    )

    def at(lon, lat):
        return lon * lats + lat

    route_a, route_b = [], []
    for lon in range(lons):
        for lat in range(lats):
            other = lat + 1 if lat % 2 == 0 else lat - 1
            route_a.append((at(lon, lat), at(lon, other)))
            if lat == lats - 1:
                route_b.append((at(lon, lat), at(lons - 1 - lon, lat)))
            elif lat > 0:
                other = lat - 1 if lat % 2 == 0 else lat + 1
                route_b.append((at(lon, lat), at(lon, other)))
    got_a = lax.ppermute(rows_a, ("lon", "lat"), route_a)
    got_b = lax.ppermute(rows_b, ("lon", "lat"), route_b)
    full_p = lax.ppermute(full, "lev", swap)
    got_a_p = lax.ppermute(got_a, "lev", swap)
    got_b_p = lax.ppermute(got_b, "lev", swap)

    (out,) = call(
        steps_kernel,
        [(2, 3, 128, 128)],
        [
            (2, 7, R, 128), (2, 7, R, 128), (7, R, 128), (5, 9, R, 128), (5, 4, 8, 128),
            (9, R, 128), (R, 128), (R, 128), (9, R, 128), (4, 8, 128), (R, 128), (R, 128), (2, 4, R, 128),
        ],
    )(*blocks, lev_in, full, full_p, got_a, got_b, got_a_p, got_b_p)
    return out


def solution(mesh):
    return jax.shard_map(
        local,
        mesh=mesh,
        in_specs=(
            P("members", "lev", "lat", "lon"),
            P("lev", "lat", "lon"),
            P("members", "lev", "lat", "lon"),
            P("members", "lev", "lat", "lon"),
        ),
        out_specs=P("members", "lev", "lat", "lon"),
        check_vma=False,
    )
```

```python
import jax
import jax.numpy as jnp
from jax import lax
from jax.experimental import pallas as pl
from jax.experimental.pallas import tpu as pltpu
from jax.sharding import PartitionSpec as P

STEPS = 3
S0, EV, S1, ED, ES, NV, ND, NS, WET = range(9)
R = 136
VMEM = pl.BlockSpec(memory_space=pltpu.VMEM)
PARAMS = pltpu.CompilerParams(vmem_limit_bytes=40 * 2**20)
f32 = jnp.float32


def iota(shape, dim):
    return lax.broadcasted_iota(jnp.int32, shape, dim)


def roll(x, shift, axis):
    shift %= x.shape[axis]
    return x if shift == 0 else pltpu.roll(x, shift, axis)


def position():
    lev = lax.axis_index("lev")
    lat = lax.axis_index("lat")
    odd = lax.rem(lat, 2) == 1
    last = lat == lax.axis_size("lat") - 1
    return lev, odd, last


def level(q, lev):
    return q + lev * (2 - 2 * q)


def raw(refs, n, kk, rows):
    tr, ls, fe, fn = refs
    if n == WET:
        return ls[kk, rows].astype(f32)
    if n in (S0, S1):
        return tr[n // 2, kk, rows]
    if n in (EV, ED, ES):
        return fe[(EV, ED, ES).index(n), kk, rows]
    return fn[n - NV, kk, rows]


def edges_kernel(tr, ls, fe, fn, tr_v, ls_v, fe_v, fn_v, east_ref, west_ref, edge_ref, sem):
    lev, _, _ = position()
    lane = iota((8, 128), 1)
    m = lane % 10
    sources, targets = (tr, ls, fe, fn), (tr_v, ls_v, fe_v, fn_v)
    copies = []
    for i in range(3):
        copies.append([])
        for n in range(4 * i, min(4 * i + 4, 9)):
            if n == WET:
                which, lead = 1, ()
            elif n in (S0, S1):
                which, lead = 0, (n // 2,)
            elif n in (EV, ED, ES):
                which, lead = 2, ((EV, ED, ES).index(n),)
            else:
                which, lead = 3, (n - NV,)
            source, target = sources[which], targets[which]
            if lead:
                source, target = source.at[lead[0]], target.at[lead[0]]
            copy = pltpu.make_async_copy(source, target, sem.at[n])
            copy.start()
            copies[i].append(copy)
    for i in range(3):
        for copy in copies[i]:
            copy.wait()
        for t in range(16):
            rows = pl.ds(8 * t, 8)
            packed = jnp.zeros((8, 128), f32)
            for n in range(4 * i, min(4 * i + 4, 9)):
                for q in range(3):
                    x = raw(targets, n, level(q, lev), rows)
                    at = 30 * (n % 4) + 10 * q + 3 * i
                    packed = jnp.where((lane >= at) & (lane < at + 6), roll(x, at - 125, 1), packed)
            edge_ref[i, rows] = packed
    for t in range(16):
        rows = pl.ds(8 * t, 8)
        a, b, c = edge_ref[0, rows], edge_ref[1, rows], edge_ref[2, rows]
        east_ref[rows] = jnp.where(m < 3, a, jnp.where(m < 6, b, c))
        west_ref[rows] = jnp.where((m >= 3) & (m < 6), a, jnp.where((m >= 6) & (m < 9), b, c))


def planes_kernel(tr, ls, fe, fn, lev_ref, a_ref, b_ref):
    refs = (tr, ls, fe, fn)
    lev, odd, last = position()
    lane = iota((8, 128), 1)
    sub = iota((8, 128), 0)
    for q in range(3):
        kk = level(q, lev)
        for c in range(2):
            lev_ref[3 * c + q] = tr[c, kk]
        lev_ref[6 + q] = ls[kk].astype(f32)
        if q >= 1:
            for face in range(3):
                lev_ref[9 + face * 2 + q - 1] = fe[face, kk]
                lev_ref[15 + face * 2 + q - 1] = fn[face, kk]

    def ends(p):
        if p >= 27:
            return (jnp.zeros((8, 128), f32),) * 2
        n, q = divmod(p, 3)
        kk = level(q, lev)
        return raw(refs, n, kk, pl.ds(120, 8)), raw(refs, n, kk, pl.ds(0, 8))

    for j in range(17):
        n, n2 = j // 3, (j + 17) // 3
        top, bottom = ends(j)
        top2, bottom2 = ends(j + 17)
        as_south = jnp.where(sub >= 4, top, roll(top2, 4, 0))
        as_north = jnp.where(sub < 4, bottom, roll(bottom2, 4, 0))
        folded = jnp.take_along_axis(jnp.take_along_axis(as_south, 7 - sub, axis=0), 127 - lane, axis=1)
        if n in (EV, ED, ES):
            folded = jnp.where(sub < 4, roll(folded, -1, 1), folded)
        if n in (EV, ES, NV, NS):
            folded = jnp.where(sub < 4, -folded, folded)
        if n2 in (NV, NS):
            folded = jnp.where(sub >= 4, -folded, folded)
        a_ref[j] = jnp.where(odd, as_north, as_south)
        b_ref[j] = jnp.where(odd, jnp.where(last, folded, as_south), as_north)


def rows_kernel(strip, from_east, from_west, a_in, b_in, full_ref, a_ref, b_ref):
    lev, odd, last = position()
    m = iota((128, 128), 1) % 10
    e, w = from_east[...], from_west[...]
    for i in range(3):
        full_ref[0, i] = jnp.where((m >= 6) & (m < 9), roll(e, 3 - 3 * i, 1), strip[0, i])
        full_ref[1, i] = jnp.where(m < 3, roll(w, -3 * i, 1), strip[1, i])
    lane = iota((8, 128), 1)
    sub = iota((8, 128), 0)
    m = lane % 10
    group = lane - m
    quarter = lane // 30
    for j in range(17):
        if not 10 <= j < 16:
            a_ref[j] = a_in[j]
            b_ref[j] = b_in[j]
    turned = []
    for j in range(10, 16):
        side, i = divmod(j - 10, 3)
        top, bottom = full_ref[side, i, pl.ds(120, 8)], full_ref[side, i, pl.ds(0, 8)]
        swapped = jnp.take_along_axis(full_ref[1 - side, i, pl.ds(120, 8)], 7 - sub, axis=0)
        if side == 0:
            turned.append(swapped)
        east_item = [(quarter == 1) | (quarter == 3), quarter == 0, quarter < 0][i]
        negative = [quarter == 1, (quarter == 0) | (quarter == 1) | (quarter == 3), quarter < 0][i]
        source = jnp.clip(group + jnp.where(east_item, 7, 8) - m, 0, 127)
        folded = jnp.take_along_axis(swapped, source, axis=1)
        folded = jnp.where(negative, -folded, folded)
        as_south, as_north, folded = roll(top, 4, 0), roll(bottom, 4, 0), roll(folded, 4, 0)
        a_ref[j] = jnp.where(
            odd, jnp.where(sub < 4, a_in[j], as_north), jnp.where(sub >= 4, a_in[j], as_south)
        )
        b_south = jnp.where(sub >= 4, b_in[j], as_south)
        b_north = jnp.where(sub < 4, b_in[j], jnp.where(last, folded, as_north))
        b_ref[j] = jnp.where(jnp.logical_and(odd, jnp.logical_not(last)), b_south, b_north)
    for n in (EV, ED, ES):
        for q in range(3):
            j = 3 * n + q
            at = 30 * (n % 4) + 10 * q + 2
            x = roll(turned[n // 4], 127 - at, 1)
            x = x if n == ED else -x
            b_ref[j] = jnp.where((lane == 127) & (sub < 4) & last, x, b_ref[j])


def coefficients(v, d, slope, wet):
    return (
        wet * (jnp.maximum(v, 0.0) + d),
        wet * (jnp.minimum(v, 0.0) - d),
        wet * (d * 0.25 * slope),
    )


def tile(t):
    return pl.ds(8 * t, 8)


def rows_up(sub, here, above):
    return jnp.where(sub == 7, roll(above, -1, 0), roll(here, -1, 0))


def rows_down(sub, here, below):
    return jnp.where(sub == 0, roll(below, 1, 0), roll(here, 1, 0))


def north_coefficients(ring, v, d, s, wet, put, far=None):
    sub = iota((8, 128), 0)
    size = len(ring)
    known = {}
    for at in [size - 1] + list(range(size)):
        t = ring[at]
        if t not in known:
            wet_t = wet(t) * rows_up(sub, wet(t), wet(ring[(at + 1) % size]))
            known[t] = coefficients(v(t), d(t), s(t), wet_t)
            if far and t == 15:
                x, y, z = coefficients(*(roll(f, -1, 0) for f in far[:3]), wet_t)
                beyond = jnp.logical_and(far[3], sub == 7)
                a2, b2, c2 = (jnp.where(beyond, f, g) for f, g in zip((x, y, z), known[t]))
                far[4](0, a2)
                far[4](1, c2)
        below = known.get(ring[at - 1])
        if below is not None:
            a, b, c = known[t]
            put(t, 4, a)
            put(t, 5, c)
            put(t, 6, rows_down(sub, b, below[1]))
            put(t, 7, rows_down(sub, c, below[2]))
            if far and t == 16:
                far[4](2, rows_down(sub, b, b2))
                far[4](3, rows_down(sub, c, c2))


def terms(ring, coef, coef2, state, vertical, push, skip=()):
    sub = iota((8, 128), 0)
    size = len(ring)
    held = {}

    def make(t):
        s, u = state(t), vertical(t)
        up_face = coef(t, 4) * s + coef(t, 5) * u
        down_face = coef(t, 6) * s + coef(t, 7) * u
        far, near = up_face, down_face
        if coef2 and t == 15:
            far = coef2(0) * s + coef2(1) * u
        if coef2 and t == 16:
            near = coef2(2) * s + coef2(3) * u
        part = None
        if t not in skip:
            east, west = coef(t, 0) * s + coef(t, 1) * u, coef(t, 2) * s + coef(t, 3) * u
            push(t, east, west)
            part = s + (west - east) + (near - up_face)
        held[t] = part, up_face, far, down_face

    make(ring[-1])
    make(ring[0])
    for at, t in enumerate(ring):
        if at + 1 < size - 1:
            make(ring[at + 1])
        if t in skip:
            continue
        part, up_face, _, down_face = held[t]
        x = rows_down(sub, up_face, held[ring[at - 1]][2])
        y = rows_up(sub, down_face, held[ring[(at + 1) % size]][3])
        yield t, part + (x - y)


def block_kernel(tr, ls, fe, fn, lev_in, out, strip_ref, SA, SB, W, K, D):
    lev, _, _ = position()
    refs = (tr, ls, fe, fn)
    lane = iota((8, 128), 1)
    ring = list(range(16))
    half = jnp.where(lev == 0, 0.5, -0.5)
    zero = jnp.zeros((128, 128), f32)

    for t in ring:
        for i in range(3):
            east = west = jnp.zeros((8, 128), f32)
            for n in range(4 * i, min(4 * i + 4, 9)):
                for q in range(3):
                    x = raw(refs, n, level(q, lev), tile(t))
                    at = 30 * (n % 4) + 10 * q
                    east = jnp.where((lane >= at) & (lane < at + 6), roll(x, at - 122, 1), east)
                    west = jnp.where((lane >= at + 3) & (lane < at + 9), roll(x, at + 3, 1), west)
            strip_ref[0, i, tile(t)] = east
            strip_ref[1, i, tile(t)] = west

    for c in range(2):
        SA[c, 0] = zero
        SB[c, 0] = zero
    W[0] = zero
    for q in range(3):
        kk = level(q, lev)
        for c in range(2):
            SA[c, q + 1] = tr[c, kk]
            SA[c, 6 - q] = lev_in[3 * c + q]
        W[q + 1] = ls[kk].astype(f32)
        W[6 - q] = lev_in[6 + q]

    for q in range(5):
        kk = level(min(q, 2), lev)

        def field(n, t):
            if q >= 3:
                return lev_in[9 + (EV, ED, ES, NV, ND, NS).index(n) * 2 + 4 - q, tile(t)]
            return raw(refs, n, kk, tile(t))

        for t in ring:
            wet = W[q + 1, tile(t)]
            D[0, 0, tile(t)] = wet * roll(wet, -1, 1)
            K[q, 8, tile(t)] = half * W[q, tile(t)] * wet * W[q + 2, tile(t)]
        for t in ring:
            a, b, c = coefficients(field(EV, t), field(ED, t), field(ES, t), D[0, 0, tile(t)])
            K[q, 0, tile(t)] = a
            K[q, 1, tile(t)] = c
            K[q, 2, tile(t)] = roll(b, 1, 1)
            K[q, 3, tile(t)] = roll(c, 1, 1)

        def put(t, at, x):
            K[q, at, tile(t)] = x

        north_coefficients(
            ring, lambda t: field(NV, t), lambda t: field(ND, t), lambda t: field(NS, t),
            lambda t: W[q + 1, tile(t)], put,
        )

    for step in range(STEPS):
        now, later = (SA, SB) if step % 2 == 0 else (SB, SA)

        @pl.loop(0, 5 - step)
        def _(q):
            for c in range(2):
                def push(t, east, west):
                    D[c, 0, tile(t)] = roll(east, 1, 1)
                    D[c, 1, tile(t)] = roll(west, -1, 1)

                def vertical(t):
                    return K[q, 8, tile(t)] * (now[c, q + 2, tile(t)] - now[c, q, tile(t)])

                for t, part in terms(
                    ring, lambda t, i: K[q, i, tile(t)], None,
                    lambda t: now[c, q + 1, tile(t)], vertical, push,
                ):
                    D[c, 2, tile(t)] = part
            for c in range(2):
                for t in ring:
                    x = D[c, 2, tile(t)] + (D[c, 0, tile(t)] - D[c, 1, tile(t)])
                    if step == STEPS - 1:
                        out[c, level(q, lev), tile(t)] = x
                    else:
                        later[c, q + 1, tile(t)] = x


def frame_kernel(
    tr, ls, fe, fn, lev_in, block, strip_o, strip_p, a_o, b_o, a_p, b_p,
    out, SA, SB, W, K, K2, D, F, SK, SK2, SS0, SS1, U, DS, whole, sem,
):
    lev, odd, last = position()
    refs = (tr, ls, fe, fn)
    lane = iota((8, 128), 1)
    sub = iota((8, 128), 0)
    half = jnp.where(lev == 0, 0.5, -0.5)
    every = list(range(17))
    ring = [15, 16, 0]
    spot = {15: pl.ds(0, 8), 16: pl.ds(8, 8), 0: pl.ds(16, 8)}

    def halo(p, partner):
        a, b = (a_p, b_p) if partner else (a_o, b_o)
        x, y = a[p % 17], b[p % 17]
        north, south = jnp.where(odd, y, x), jnp.where(odd, x, y)
        if p >= 17:
            north, south = roll(north, 4, 0), roll(south, 4, 0)
        return north, jnp.where(sub >= 5, south, 0.0)

    def joined(n, north, south):
        if n in (NV, ND, NS):
            return jnp.where(sub < 2, jnp.where(last, roll(north, -1, 0), north), south)
        return jnp.where(sub < 3, north, south)

    zero = jnp.zeros((24, 128), f32)
    for c in range(2):
        SA[c, 0] = zero
        SB[c, 0] = zero
    W[0] = zero
    for q in range(3):
        kk = level(q, lev)
        for t in (15, 0):
            for c in range(2):
                SA[c, q + 1, spot[t]] = tr[c, kk, tile(t)]
                SA[c, 6 - q, spot[t]] = lev_in[3 * c + q, tile(t)]
            W[q + 1, spot[t]] = ls[kk, tile(t)].astype(f32)
            W[6 - q, spot[t]] = lev_in[6 + q, tile(t)]
        for c in range(2):
            SA[c, q + 1, spot[16]] = joined(S0, *halo(3 * (S0, S1)[c] + q, False))
            SA[c, 6 - q, spot[16]] = joined(S0, *halo(3 * (S0, S1)[c] + q, True))
        W[q + 1, spot[16]] = joined(WET, *halo(3 * WET + q, False))
        W[6 - q, spot[16]] = joined(WET, *halo(3 * WET + q, True))

    def rows_coefficients(q):
        partner = q >= 3
        qq = 5 - q if partner else q
        kk = level(qq, lev)

        def field(n, t):
            if t == 16:
                return joined(n, *halo(3 * n + qq, partner))
            if partner:
                return lev_in[9 + (EV, ED, ES, NV, ND, NS).index(n) * 2 + qq - 1, tile(t)]
            return raw(refs, n, kk, tile(t))

        for t in ring:
            wet = W[q + 1, spot[t]]
            a, b, c = coefficients(field(EV, t), field(ED, t), field(ES, t), wet * roll(wet, -1, 1))
            K[q, 0, spot[t]] = a
            K[q, 1, spot[t]] = c
            K[q, 2, spot[t]] = roll(b, 1, 1)
            K[q, 3, spot[t]] = roll(c, 1, 1)
            K[q, 8, spot[t]] = half * W[q, spot[t]] * wet * W[q + 2, spot[t]]

        def put(t, at, x):
            K[q, at, spot[t]] = x

        def put2(at, x):
            K2[q, at] = x

        north_coefficients(
            ring, lambda t: field(NV, t), lambda t: field(ND, t), lambda t: field(NS, t),
            lambda t: W[q + 1, spot[t]], put,
            (*(halo(3 * n + qq, partner)[0] for n in (NV, ND, NS)), last, put2),
        )

    def rows_step(step, q):
        now = SA if step % 2 == 0 else SB
        for c in range(2):
            def push(t, east, west):
                D[q, c, 0, spot[t]] = roll(east, 1, 1)
                D[q, c, 1, spot[t]] = roll(west, -1, 1)

            def vertical(t):
                return K[q, 8, spot[t]] * (now[c, q + 2, spot[t]] - now[c, q, spot[t]])

            for t, part in terms(
                ring, lambda t, i: K[q, i, spot[t]], lambda i: K2[q, i],
                lambda t: now[c, q + 1, spot[t]], vertical, push,
            ):
                D[q, c, 2, spot[t]] = part

    def rows_update(step):
        later = SB if step % 2 == 0 else SA
        for q in range(5 - step):
            for c in range(2):
                later[c, q + 1] = D[q, c, 2] + (D[q, c, 0] - D[q, c, 1])

    m = lane % 10
    group = lane // 10
    q_here = group % 6
    mine = q_here < 3
    used = (lane < 120) & (m < 9)
    own_at = 10 * q_here + m
    partner_at = 10 * (5 - q_here) + m
    far = [[None] * 3, [None] * 3]

    def spread(side):
        for n in range(9):
            if n == S1:
                continue
            index = jnp.where(mine, own_at, partner_at)
            index = index + (jnp.where(group >= 6, 60, 0) if n == S0 else 30 * (n % 4))
            index = jnp.clip(index, 0, 127)
            i = n // 4

            def pick(x, y):
                x = jnp.take_along_axis(x, index, axis=1)
                y = jnp.take_along_axis(y, index, axis=1)
                return jnp.where(used, jnp.where(mine, x, y), 0.0)

            for t in range(16):
                F[side, n, tile(t)] = pick(strip_o[side, i, tile(t)], strip_p[side, i, tile(t)])
            p = 27 + 3 * side + i
            north, south = (pick(x, y) for x, y in zip(halo(p, False), halo(p, True)))
            F[side, n, tile(16)] = joined(n, north, south)
            if n in (NV, ND, NS):
                far[side][n - NV] = north

    def strip_faces(side):
        outside = (q_here == 0) | (q_here == 5)
        for t in every:
            wet = F[side, WET, tile(t)]
            DS[side, 0, tile(t)] = wet * roll(wet, -1, 1)
            around = roll(wet, -10, 1) * roll(wet, 10, 1)
            SK[side, 8, tile(t)] = jnp.where(outside, 0.0, half * wet * around)
            SS0[side, tile(t)] = F[side, S0, tile(t)]

    def strip_coefficients(side):
        for t in every:
            a, b, c = coefficients(*(F[side, n, tile(t)] for n in (EV, ED, ES)), DS[side, 0, tile(t)])
            SK[side, 0, tile(t)] = a
            SK[side, 1, tile(t)] = c
            SK[side, 2, tile(t)] = roll(b, 1, 1)
            SK[side, 3, tile(t)] = roll(c, 1, 1)

        def put(t, at, x):
            SK[side, at, tile(t)] = x

        def put2(at, x):
            SK2[side, at] = x

        north_coefficients(
            every, *(lambda t, n=n: F[side, n, tile(t)] for n in (NV, ND, NS, WET)), put,
            (*far[side], last, put2),
        )

    def strip_vertical(step, side):
        now = SS0 if step % 2 == 0 else SS1
        for t in every:
            s = now[side, tile(t)]
            U[side, tile(t)] = SK[side, 8, tile(t)] * (roll(s, -10, 1) - roll(s, 10, 1))

    def strip_step(step, side):
        now = SS0 if step % 2 == 0 else SS1

        def push(t, east, west):
            DS[side, 0, tile(t)] = roll(east, 1, 1)
            DS[side, 1, tile(t)] = roll(west, -1, 1)

        for t, part in terms(
            every, lambda t, i: SK[side, i, tile(t)], lambda i: SK2[side, i],
            lambda t: now[side, tile(t)], lambda t: U[side, tile(t)], push,
            (16,) if step == STEPS - 1 else (),
        ):
            DS[side, 2, tile(t)] = part

    def strip_update(step, side):
        later = SS1 if step % 2 == 0 else SS0
        for t in range(16 if step == STEPS - 1 else 17):
            later[side, tile(t)] = DS[side, 2, tile(t)] + (DS[side, 0, tile(t)] - DS[side, 1, tile(t)])

    for side in range(2):
        spread(side)
    for q in range(2):
        rows_coefficients(q)
    for side in range(2):
        strip_faces(side)
    for q in range(2, 5):
        rows_coefficients(q)
    for side in range(2):
        strip_coefficients(side)
    for step in range(STEPS):
        for side in range(2):
            strip_vertical(step, side)
        for q in range(5 - step):
            rows_step(step, q)
        for side in range(2):
            strip_step(step, side)
        rows_update(step)
        for side in range(2):
            strip_update(step, side)

    rows_last, strips_last = (SB, SS1) if STEPS % 2 else (SA, SS0)
    for t in range(16):
        U[0, tile(t)] = jnp.where(m < 3, roll(strips_last[0, tile(t)], -3, 1), strips_last[1, tile(t)])
    copies = []
    for c in range(2):
        for q in range(3):
            kk = level(q, lev)
            for t in range(16):
                x = block[c, kk, tile(t)]
                if t == 0:
                    x = jnp.where(sub < 3, rows_last[c, q + 1, spot[0]], x)
                if t == 15:
                    x = jnp.where(sub >= 5, rows_last[c, q + 1, spot[15]], x)
                edge = roll(U[0, tile(t)], 125 - 10 * (6 * c + q), 1)
                whole[c, kk, tile(t)] = jnp.where((lane < 3) | (lane >= 125), edge, x)
            copy = pltpu.make_async_copy(whole.at[c, kk], out.at[c, kk], sem.at[3 * c + q])
            copy.start()
            copies.append(copy)
    for copy in copies:
        copy.wait()


FRAME_SCRATCH = [
    (2, 7, 24, 128), (2, 7, 24, 128), (7, 24, 128), (5, 9, 24, 128), (5, 4, 8, 128), (5, 2, 3, 24, 128),
    (2, 9, R, 128), (2, 9, R, 128), (2, 4, 8, 128), (2, R, 128), (2, R, 128), (2, R, 128), (2, 3, R, 128),
    (2, 3, 128, 128), pltpu.SemaphoreType.DMA((6,)),
]


def call(kernel, shapes, scratch=(), types=(), in_specs=None, out_spec=VMEM, cost=None):
    types = list(types) + [f32] * (len(shapes) - len(types))
    return pl.pallas_call(
        kernel,
        out_shape=[jax.ShapeDtypeStruct(s, d) for s, d in zip(shapes, types)],
        **({} if in_specs is None else dict(in_specs=in_specs)),
        out_specs=[out_spec] * len(shapes),
        scratch_shapes=[pltpu.VMEM(s, f32) if isinstance(s, tuple) else s for s in scratch],
        compiler_params=PARAMS,
        cost_estimate=cost and pl.CostEstimate(flops=cost, bytes_accessed=cost, transcendentals=0),
    )


def local(tracers, land_sea, faces_east, faces_north):
    lons, lats = lax.axis_size("lon"), lax.axis_size("lat")
    swap = [(0, 1), (1, 0)]

    inputs = (tracers, land_sea, faces_east, faces_north)
    hbm = pl.BlockSpec(memory_space=pltpu.HBM)
    *blocks, to_east, to_west = call(
        edges_kernel,
        [x.shape for x in inputs] + [(128, 128), (128, 128)],
        [(3, 128, 128), pltpu.SemaphoreType.DMA((9,))],
        types=[x.dtype for x in inputs],
        in_specs=[hbm] * 4,
    )(*[pltpu.with_memory_space_constraint(x, pltpu.HBM) for x in inputs])
    from_west = lax.ppermute(to_east, "lon", [(i, (i + 1) % lons) for i in range(lons)])
    from_east = lax.ppermute(to_west, "lon", [((i + 1) % lons, i) for i in range(lons)])
    levels, rows_a, rows_b = call(planes_kernel, [(21, 128, 128), (17, 8, 128), (17, 8, 128)])(*blocks)
    lev_in = lax.ppermute(levels, "lev", swap)
    block, strip = call(
        block_kernel,
        [(2, 3, 128, 128), (2, 3, 128, 128)],
        [(2, 7, 128, 128), (2, 7, 128, 128), (7, 128, 128), (5, 9, 128, 128), (2, 3, 128, 128)],
        cost=20_000_000,
    )(*blocks, lev_in)
    full, rows_a, rows_b = call(rows_kernel, [(2, 3, 128, 128), (17, 8, 128), (17, 8, 128)])(
        strip, from_east, from_west, rows_a, rows_b
    )

    def at(lon, lat):
        return lon * lats + lat

    route_a, route_b = [], []
    for lon in range(lons):
        for lat in range(lats):
            other = lat + 1 if lat % 2 == 0 else lat - 1
            route_a.append((at(lon, lat), at(lon, other)))
            if lat == lats - 1:
                route_b.append((at(lon, lat), at(lons - 1 - lon, lat)))
            elif lat > 0:
                other = lat - 1 if lat % 2 == 0 else lat + 1
                route_b.append((at(lon, lat), at(lon, other)))
    got_a = lax.ppermute(rows_a, ("lon", "lat"), route_a)
    got_b = lax.ppermute(rows_b, ("lon", "lat"), route_b)
    full_p = lax.ppermute(full, "lev", swap)
    got_a_p = lax.ppermute(got_a, "lev", swap)
    got_b_p = lax.ppermute(got_b, "lev", swap)

    (out,) = call(
        frame_kernel,
        [(2, 3, 128, 128)],
        FRAME_SCRATCH,
        out_spec=hbm,
    )(*blocks, lev_in, block, full, full_p, got_a, got_b, got_a_p, got_b_p)
    return out


def solution(mesh):
    return jax.shard_map(
        local,
        mesh=mesh,
        in_specs=(
            P("members", "lev", "lat", "lon"),
            P("lev", "lat", "lon"),
            P("members", "lev", "lat", "lon"),
            P("members", "lev", "lat", "lon"),
        ),
        out_specs=P("members", "lev", "lat", "lon"),
        check_vma=False,
    )
```

```python
import jax
import jax.numpy as jnp
from jax import lax
from jax.experimental import pallas as pl
from jax.experimental.pallas import tpu as pltpu
from jax.sharding import PartitionSpec as P

STEPS = 3
S0, EV, S1, ED, ES, NV, ND, NS, WET = range(9)
R = 136
VMEM = pl.BlockSpec(memory_space=pltpu.VMEM)
PARAMS = pltpu.CompilerParams(vmem_limit_bytes=40 * 2**20)
f32 = jnp.float32


def iota(shape, dim):
    return lax.broadcasted_iota(jnp.int32, shape, dim)


def roll(x, shift, axis):
    shift %= x.shape[axis]
    return x if shift == 0 else pltpu.roll(x, shift, axis)


def position():
    lev = lax.axis_index("lev")
    lat = lax.axis_index("lat")
    odd = lax.rem(lat, 2) == 1
    last = lat == lax.axis_size("lat") - 1
    return lev, odd, last


def level(q, lev):
    return q + lev * (2 - 2 * q)


def raw(refs, n, kk, rows):
    tr, ls, fe, fn = refs
    if n == WET:
        return ls[kk, rows].astype(f32)
    if n in (S0, S1):
        return tr[n // 2, kk, rows]
    if n in (EV, ED, ES):
        return fe[(EV, ED, ES).index(n), kk, rows]
    return fn[n - NV, kk, rows]


def edges_kernel(tr, ls, fe, fn, tr_v, ls_v, fe_v, fn_v, east_ref, west_ref, edge_ref, sem):
    lev, _, _ = position()
    lane = iota((8, 128), 1)
    m = lane % 10
    sources, targets = (tr, ls, fe, fn), (tr_v, ls_v, fe_v, fn_v)
    copies = []
    for i in range(3):
        copies.append([])
        for n in range(4 * i, min(4 * i + 4, 9)):
            if n == WET:
                which, lead = 1, ()
            elif n in (S0, S1):
                which, lead = 0, (n // 2,)
            elif n in (EV, ED, ES):
                which, lead = 2, ((EV, ED, ES).index(n),)
            else:
                which, lead = 3, (n - NV,)
            source, target = sources[which], targets[which]
            if lead:
                source, target = source.at[lead[0]], target.at[lead[0]]
            copy = pltpu.make_async_copy(source, target, sem.at[n])
            copy.start()
            copies[i].append(copy)
    for i in range(3):
        for copy in copies[i]:
            copy.wait()
        for t in range(16):
            rows = pl.ds(8 * t, 8)
            packed = jnp.zeros((8, 128), f32)
            for n in range(4 * i, min(4 * i + 4, 9)):
                for q in range(3):
                    x = raw(targets, n, level(q, lev), rows)
                    at = 30 * (n % 4) + 10 * q + 3 * i
                    packed = jnp.where((lane >= at) & (lane < at + 6), roll(x, at - 125, 1), packed)
            edge_ref[i, rows] = packed
    for t in range(16):
        rows = pl.ds(8 * t, 8)
        a, b, c = edge_ref[0, rows], edge_ref[1, rows], edge_ref[2, rows]
        east_ref[rows] = jnp.where(m < 3, a, jnp.where(m < 6, b, c))
        west_ref[rows] = jnp.where((m >= 3) & (m < 6), a, jnp.where((m >= 6) & (m < 9), b, c))


def planes_kernel(tr, ls, fe, fn, lev_ref, a_ref, b_ref):
    refs = (tr, ls, fe, fn)
    lev, odd, last = position()
    lane = iota((8, 128), 1)
    sub = iota((8, 128), 0)
    for q in range(3):
        kk = level(q, lev)
        for c in range(2):
            lev_ref[3 * c + q] = tr[c, kk]
        lev_ref[6 + q] = ls[kk].astype(f32)
        if q >= 1:
            for face in range(3):
                lev_ref[9 + face * 2 + q - 1] = fe[face, kk]
                lev_ref[15 + face * 2 + q - 1] = fn[face, kk]

    def ends(p):
        if p >= 27:
            return (jnp.zeros((8, 128), f32),) * 2
        n, q = divmod(p, 3)
        kk = level(q, lev)
        return raw(refs, n, kk, pl.ds(120, 8)), raw(refs, n, kk, pl.ds(0, 8))

    for j in range(17):
        n, n2 = j // 3, (j + 17) // 3
        top, bottom = ends(j)
        top2, bottom2 = ends(j + 17)
        as_south = jnp.where(sub >= 4, top, roll(top2, 4, 0))
        as_north = jnp.where(sub < 4, bottom, roll(bottom2, 4, 0))
        folded = jnp.take_along_axis(jnp.take_along_axis(as_south, 7 - sub, axis=0), 127 - lane, axis=1)
        if n in (EV, ED, ES):
            folded = jnp.where(sub < 4, roll(folded, -1, 1), folded)
        if n in (EV, ES, NV, NS):
            folded = jnp.where(sub < 4, -folded, folded)
        if n2 in (NV, NS):
            folded = jnp.where(sub >= 4, -folded, folded)
        a_ref[j] = jnp.where(odd, as_north, as_south)
        b_ref[j] = jnp.where(odd, jnp.where(last, folded, as_south), as_north)


def rows_kernel(strip, from_east, from_west, a_in, b_in, full_ref, a_ref, b_ref):
    lev, odd, last = position()
    m = iota((128, 128), 1) % 10
    e, w = from_east[...], from_west[...]
    for i in range(3):
        full_ref[0, i] = jnp.where((m >= 6) & (m < 9), roll(e, 3 - 3 * i, 1), strip[0, i])
        full_ref[1, i] = jnp.where(m < 3, roll(w, -3 * i, 1), strip[1, i])
    lane = iota((8, 128), 1)
    sub = iota((8, 128), 0)
    m = lane % 10
    group = lane - m
    quarter = lane // 30
    for j in range(17):
        if not 10 <= j < 16:
            a_ref[j] = a_in[j]
            b_ref[j] = b_in[j]
    turned = []
    for j in range(10, 16):
        side, i = divmod(j - 10, 3)
        top, bottom = full_ref[side, i, pl.ds(120, 8)], full_ref[side, i, pl.ds(0, 8)]
        swapped = jnp.take_along_axis(full_ref[1 - side, i, pl.ds(120, 8)], 7 - sub, axis=0)
        if side == 0:
            turned.append(swapped)
        east_item = [(quarter == 1) | (quarter == 3), quarter == 0, quarter < 0][i]
        negative = [quarter == 1, (quarter == 0) | (quarter == 1) | (quarter == 3), quarter < 0][i]
        source = jnp.clip(group + jnp.where(east_item, 7, 8) - m, 0, 127)
        folded = jnp.take_along_axis(swapped, source, axis=1)
        folded = jnp.where(negative, -folded, folded)
        as_south, as_north, folded = roll(top, 4, 0), roll(bottom, 4, 0), roll(folded, 4, 0)
        a_ref[j] = jnp.where(
            odd, jnp.where(sub < 4, a_in[j], as_north), jnp.where(sub >= 4, a_in[j], as_south)
        )
        b_south = jnp.where(sub >= 4, b_in[j], as_south)
        b_north = jnp.where(sub < 4, b_in[j], jnp.where(last, folded, as_north))
        b_ref[j] = jnp.where(jnp.logical_and(odd, jnp.logical_not(last)), b_south, b_north)
    for n in (EV, ED, ES):
        for q in range(3):
            j = 3 * n + q
            at = 30 * (n % 4) + 10 * q + 2
            x = roll(turned[n // 4], 127 - at, 1)
            x = x if n == ED else -x
            b_ref[j] = jnp.where((lane == 127) & (sub < 4) & last, x, b_ref[j])


def coefficients(v, d, slope, wet):
    return (
        wet * (jnp.maximum(v, 0.0) + d),
        wet * (jnp.minimum(v, 0.0) - d),
        wet * (d * 0.25 * slope),
    )


def tile(t):
    return pl.ds(8 * t, 8)


def rows_up(sub, here, above):
    return jnp.where(sub == 7, roll(above, -1, 0), roll(here, -1, 0))


def rows_down(sub, here, below):
    return jnp.where(sub == 0, roll(below, 1, 0), roll(here, 1, 0))


def north_coefficients(ring, v, d, s, wet, put, far=None):
    sub = iota((8, 128), 0)
    size = len(ring)
    known = {}
    for at in [size - 1] + list(range(size)):
        t = ring[at]
        if t not in known:
            wet_t = wet(t) * rows_up(sub, wet(t), wet(ring[(at + 1) % size]))
            known[t] = coefficients(v(t), d(t), s(t), wet_t)
            if far and t == 15:
                x, y, z = coefficients(*(roll(f, -1, 0) for f in far[:3]), wet_t)
                beyond = jnp.logical_and(far[3], sub == 7)
                a2, b2, c2 = (jnp.where(beyond, f, g) for f, g in zip((x, y, z), known[t]))
                far[4](0, a2)
                far[4](1, c2)
        below = known.get(ring[at - 1])
        if below is not None:
            a, b, c = known[t]
            put(t, 4, a)
            put(t, 5, c)
            put(t, 6, rows_down(sub, b, below[1]))
            put(t, 7, rows_down(sub, c, below[2]))
            if far and t == 16:
                far[4](2, rows_down(sub, b, b2))
                far[4](3, rows_down(sub, c, c2))


def terms(ring, coef, coef2, state, vertical, push, skip=()):
    sub = iota((8, 128), 0)
    size = len(ring)
    held = {}

    def make(t):
        s, u = state(t), vertical(t)
        up_face = coef(t, 4) * s + coef(t, 5) * u
        down_face = coef(t, 6) * s + coef(t, 7) * u
        far, near = up_face, down_face
        if coef2 and t == 15:
            far = coef2(0) * s + coef2(1) * u
        if coef2 and t == 16:
            near = coef2(2) * s + coef2(3) * u
        part = None
        if t not in skip:
            east, west = coef(t, 0) * s + coef(t, 1) * u, coef(t, 2) * s + coef(t, 3) * u
            push(t, east, west)
            part = s + (west - east) + (near - up_face)
        held[t] = part, up_face, far, down_face

    make(ring[-1])
    make(ring[0])
    for at, t in enumerate(ring):
        if at + 1 < size - 1:
            make(ring[at + 1])
        if t in skip:
            continue
        part, up_face, _, down_face = held[t]
        x = rows_down(sub, up_face, held[ring[at - 1]][2])
        y = rows_up(sub, down_face, held[ring[(at + 1) % size]][3])
        yield t, part + (x - y)


def block_kernel(tr, ls, fe, fn, lev_in, out, strip_ref, ends, SA, SB, W, K, D):
    lev, _, _ = position()
    refs = (tr, ls, fe, fn)
    lane = iota((8, 128), 1)
    ring = list(range(16))
    half = jnp.where(lev == 0, 0.5, -0.5)
    zero = jnp.zeros((128, 128), f32)

    for t in ring:
        for i in range(3):
            east = west = jnp.zeros((8, 128), f32)
            for n in range(4 * i, min(4 * i + 4, 9)):
                for q in range(3):
                    x = raw(refs, n, level(q, lev), tile(t))
                    at = 30 * (n % 4) + 10 * q
                    east = jnp.where((lane >= at) & (lane < at + 6), roll(x, at - 122, 1), east)
                    west = jnp.where((lane >= at + 3) & (lane < at + 9), roll(x, at + 3, 1), west)
            strip_ref[0, i, tile(t)] = east
            strip_ref[1, i, tile(t)] = west

    for c in range(2):
        SA[c, 0] = zero
        SB[c, 0] = zero
    W[0] = zero
    for q in range(3):
        kk = level(q, lev)
        for c in range(2):
            SA[c, q + 1] = tr[c, kk]
            SA[c, 6 - q] = lev_in[3 * c + q]
        W[q + 1] = ls[kk].astype(f32)
        W[6 - q] = lev_in[6 + q]

    for q in range(5):
        kk = level(min(q, 2), lev)

        def field(n, t):
            if q >= 3:
                return lev_in[9 + (EV, ED, ES, NV, ND, NS).index(n) * 2 + 4 - q, tile(t)]
            return raw(refs, n, kk, tile(t))

        for t in ring:
            wet = W[q + 1, tile(t)]
            D[0, 0, tile(t)] = wet * roll(wet, -1, 1)
            K[q, 8, tile(t)] = half * W[q, tile(t)] * wet * W[q + 2, tile(t)]
        for t in ring:
            a, b, c = coefficients(field(EV, t), field(ED, t), field(ES, t), D[0, 0, tile(t)])
            K[q, 0, tile(t)] = a
            K[q, 1, tile(t)] = c
            K[q, 2, tile(t)] = roll(b, 1, 1)
            K[q, 3, tile(t)] = roll(c, 1, 1)

        def put(t, at, x):
            K[q, at, tile(t)] = x

        north_coefficients(
            ring, lambda t: field(NV, t), lambda t: field(ND, t), lambda t: field(NS, t),
            lambda t: W[q + 1, tile(t)], put,
        )
        for k in (0, 1, 2, 3, 8):
            ends[q, k, 0] = K[q, k, tile(0)]
            ends[q, k, 1] = K[q, k, tile(15)]

    for step in range(STEPS):
        now, later = (SA, SB) if step % 2 == 0 else (SB, SA)

        @pl.loop(0, 5 - step)
        def _(q):
            for c in range(2):
                def push(t, east, west):
                    D[c, 0, tile(t)] = roll(east, 1, 1)
                    D[c, 1, tile(t)] = roll(west, -1, 1)

                def vertical(t):
                    return K[q, 8, tile(t)] * (now[c, q + 2, tile(t)] - now[c, q, tile(t)])

                for t, part in terms(
                    ring, lambda t, i: K[q, i, tile(t)], None,
                    lambda t: now[c, q + 1, tile(t)], vertical, push,
                ):
                    D[c, 2, tile(t)] = part
            for c in range(2):
                for t in ring:
                    x = D[c, 2, tile(t)] + (D[c, 0, tile(t)] - D[c, 1, tile(t)])
                    if step == STEPS - 1:
                        out[c, level(q, lev), tile(t)] = x
                    else:
                        later[c, q + 1, tile(t)] = x


class Strips:
    def __init__(self, ring, spot, lev):
        self.ring, self.spot = ring, spot
        self.half = jnp.where(lev == 0, 0.5, -0.5)
        lane = iota((8, 128), 1)
        m = lane % 10
        group = lane // 10
        self.second = group >= 6
        self.q = group % 6
        self.mine = self.q < 3
        self.used = (lane < 120) & (m < 9)
        self.index = jnp.where(self.mine, 10 * self.q + m, 10 * (5 - self.q) + m)

    def pick(self, n, own, partner):
        index = self.index + (jnp.where(self.second, 60, 0) if n == S0 else 30 * (n % 4))
        index = jnp.clip(index, 0, 127)
        x = jnp.take_along_axis(own, index, axis=1)
        y = jnp.take_along_axis(partner, index, axis=1)
        return jnp.where(self.used, jnp.where(self.mine, x, y), 0.0)

    def faces(self, side, F, SK, first, D, tiles=None):
        outside = (self.q == 0) | (self.q == 5)
        for t in tiles or self.ring:
            at = self.spot[t]
            wet = F[side, WET, at]
            D[side, 0, at] = wet * roll(wet, -1, 1)
            around = roll(wet, -10, 1) * roll(wet, 10, 1)
            SK[side, 8, at] = jnp.where(outside, 0.0, self.half * wet * around)
            first[side, at] = F[side, S0, at]

    def coefficients(self, side, F, SK, D, far=None, tiles=None):
        for t in tiles or self.ring:
            at = self.spot[t]
            a, b, c = coefficients(*(F[side, n, at] for n in (EV, ED, ES)), D[side, 0, at])
            SK[side, 0, at] = a
            SK[side, 1, at] = c
            SK[side, 2, at] = roll(b, 1, 1)
            SK[side, 3, at] = roll(c, 1, 1)

        def put(t, k, x):
            SK[side, k, self.spot[t]] = x

        north_coefficients(
            self.ring, *(lambda t, n=n: F[side, n, self.spot[t]] for n in (NV, ND, NS, WET)), put, far
        )

    def vertical(self, side, now, SK, U):
        for t in self.ring:
            at = self.spot[t]
            s = now[side, at]
            U[side, at] = SK[side, 8, at] * (roll(s, -10, 1) - roll(s, 10, 1))

    def step(self, side, now, SK, SK2, U, D):
        def push(t, east, west):
            D[side, 0, self.spot[t]] = roll(east, 1, 1)
            D[side, 1, self.spot[t]] = roll(west, -1, 1)

        for t, part in terms(
            self.ring, lambda t, k: SK[side, k, self.spot[t]],
            None if SK2 is None else lambda k: SK2[side, k],
            lambda t: now[side, self.spot[t]], lambda t: U[side, self.spot[t]], push,
        ):
            D[side, 2, self.spot[t]] = part

    def update(self, side, later, D):
        for t in self.ring:
            at = self.spot[t]
            later[side, at] = D[side, 2, at] + (D[side, 0, at] - D[side, 1, at])

    def edge(self, last_strips, at):
        m = iota((8, 128), 1) % 10
        return jnp.where(m < 3, roll(last_strips[0, at], -3, 1), last_strips[1, at])


def strip_prep_kernel(strip_o, strip_p, SK, first, ends, F, D):
    lev, _, _ = position()
    strips = Strips(list(range(16)), {t: tile(t) for t in range(16)}, lev)
    for side in range(2):
        for n in range(9):
            if n != S1:
                for t in range(16):
                    F[side, n, tile(t)] = strips.pick(
                        n, strip_o[side, n // 4, tile(t)], strip_p[side, n // 4, tile(t)]
                    )
    for side in range(2):
        strips.faces(side, F, SK, first, D)
    for side in range(2):
        strips.coefficients(side, F, SK, D)
    for side in range(2):
        for n in range(9):
            if n != S1:
                ends[side, n, 0] = F[side, n, tile(0)]
                ends[side, n, 1] = F[side, n, tile(15)]


def stack_kernel(a, b, _, both):
    both[0] = a[...]
    both[1] = b[...]


def strip_steps_kernel(SK, first, block, _, out, rims, SA, SB, U, D, whole, sem):
    lev, _, _ = position()
    lane = iota((8, 128), 1)
    strips = Strips(list(range(16)), {t: tile(t) for t in range(16)}, lev)
    now = first
    for step in range(STEPS):
        later = SB if step % 2 else SA
        for side in range(2):
            strips.vertical(side, now, SK, U)
        for side in range(2):
            strips.step(side, now, SK, None, U, D)
        for side in range(2):
            strips.update(side, later, D)
        now = later
    for t in range(16):
        U[0, tile(t)] = strips.edge(now, tile(t))
    copies = []
    for c in range(2):
        for q in range(3):
            kk = level(q, lev)
            for t in range(16):
                edge = roll(U[0, tile(t)], 125 - 10 * (6 * c + q), 1)
                whole[c, kk, tile(t)] = jnp.where((lane < 3) | (lane >= 125), edge, block[c, kk, tile(t)])
            rims[0, c, kk] = whole[c, kk, tile(0)]
            rims[1, c, kk] = whole[c, kk, tile(15)]
            copy = pltpu.make_async_copy(whole.at[c, kk], out.at[c, kk], sem.at[3 * c + q])
            copy.start()
            copies.append(copy)
    for copy in copies:
        copy.wait()


def frame_kernel(
    tr, ls, fe, fn, lev_in, rims, block_ends, strip_ends, strip_coefs, rows_o, rows_p, _,
    out, SA, SB, W, K, K2, D, F, SK, SK2, SS0, SS1, U, DS, whole, sem,
):
    lev, odd, last = position()
    refs = (tr, ls, fe, fn)
    lane = iota((8, 128), 1)
    sub = iota((8, 128), 0)
    half = jnp.where(lev == 0, 0.5, -0.5)
    ring = [15, 16, 0]
    spot = {15: pl.ds(0, 8), 16: pl.ds(8, 8), 0: pl.ds(16, 8)}

    def halo(p, partner):
        rows = rows_p if partner else rows_o
        x, y = rows[0, p % 17], rows[1, p % 17]
        north, south = jnp.where(odd, y, x), jnp.where(odd, x, y)
        if p >= 17:
            north, south = roll(north, 4, 0), roll(south, 4, 0)
        return north, jnp.where(sub >= 5, south, 0.0)

    def joined(n, north, south):
        if n in (NV, ND, NS):
            return jnp.where(sub < 2, jnp.where(last, roll(north, -1, 0), north), south)
        return jnp.where(sub < 3, north, south)

    zero = jnp.zeros((24, 128), f32)
    for c in range(2):
        SA[c, 0] = zero
        SB[c, 0] = zero
    W[0] = zero
    for q in range(3):
        kk = level(q, lev)
        for t in (15, 0):
            for c in range(2):
                SA[c, q + 1, spot[t]] = tr[c, kk, tile(t)]
                SA[c, 6 - q, spot[t]] = lev_in[3 * c + q, tile(t)]
            W[q + 1, spot[t]] = ls[kk, tile(t)].astype(f32)
            W[6 - q, spot[t]] = lev_in[6 + q, tile(t)]
        for c in range(2):
            SA[c, q + 1, spot[16]] = joined(S0, *halo(3 * (S0, S1)[c] + q, False))
            SA[c, 6 - q, spot[16]] = joined(S0, *halo(3 * (S0, S1)[c] + q, True))
        W[q + 1, spot[16]] = joined(WET, *halo(3 * WET + q, False))
        W[6 - q, spot[16]] = joined(WET, *halo(3 * WET + q, True))

    def rows_coefficients(q):
        partner = q >= 3
        qq = 5 - q if partner else q
        kk = level(qq, lev)

        def field(n, t):
            if t == 16:
                return joined(n, *halo(3 * n + qq, partner))
            if partner:
                return lev_in[9 + (EV, ED, ES, NV, ND, NS).index(n) * 2 + qq - 1, tile(t)]
            return raw(refs, n, kk, tile(t))

        for k in (0, 1, 2, 3, 8):
            K[q, k, spot[0]] = block_ends[q, k, 0]
            K[q, k, spot[15]] = block_ends[q, k, 1]
        a, b, c = coefficients(field(EV, 16), field(ED, 16), field(ES, 16), D[q, 0, 0, spot[16]])
        K[q, 0, spot[16]] = a
        K[q, 1, spot[16]] = c
        K[q, 2, spot[16]] = roll(b, 1, 1)
        K[q, 3, spot[16]] = roll(c, 1, 1)
        K[q, 8, spot[16]] = half * W[q, spot[16]] * W[q + 1, spot[16]] * W[q + 2, spot[16]]

        def put(t, at, x):
            K[q, at, spot[t]] = x

        def put2(at, x):
            K2[q, at] = x

        north_coefficients(
            ring, lambda t: field(NV, t), lambda t: field(ND, t), lambda t: field(NS, t),
            lambda t: W[q + 1, spot[t]], put,
            (*(halo(3 * n + qq, partner)[0] for n in (NV, ND, NS)), last, put2),
        )

    def rows_step(step, q):
        now = SA if step % 2 == 0 else SB
        for c in range(2):
            def push(t, east, west):
                D[q, c, 0, spot[t]] = roll(east, 1, 1)
                D[q, c, 1, spot[t]] = roll(west, -1, 1)

            def vertical(t):
                return K[q, 8, spot[t]] * (now[c, q + 2, spot[t]] - now[c, q, spot[t]])

            for t, part in terms(
                ring, lambda t, i: K[q, i, spot[t]], lambda i: K2[q, i],
                lambda t: now[c, q + 1, spot[t]], vertical, push,
            ):
                D[q, c, 2, spot[t]] = part

    def rows_update(step):
        later = SB if step % 2 == 0 else SA
        for q in range(5 - step):
            for c in range(2):
                later[c, q + 1] = D[q, c, 2] + (D[q, c, 0] - D[q, c, 1])

    strips = Strips(ring, spot, lev)
    far = [[None] * 3, [None] * 3]

    def spread(side):
        for n in range(9):
            if n == S1:
                continue
            i = n // 4
            F[side, n, spot[0]] = strip_ends[side, n, 0]
            F[side, n, spot[15]] = strip_ends[side, n, 1]
            p = 27 + 3 * side + i
            north, south = (strips.pick(n, x, y) for x, y in zip(halo(p, False), halo(p, True)))
            F[side, n, spot[16]] = joined(n, north, south)
            if n in (NV, ND, NS):
                far[side][n - NV] = north
        for t in (0, 15):
            SS0[side, spot[t]] = F[side, S0, spot[t]]
            for k in (0, 1, 2, 3, 8):
                SK[side, k, spot[t]] = strip_coefs[side, k, tile(t)]

    def put_far(side):
        def put(k, x):
            SK2[side, k] = x
        return (*far[side], last, put)

    for q in range(5):
        wet = W[q + 1, spot[16]]
        D[q, 0, 0, spot[16]] = wet * roll(wet, -1, 1)
    for side in range(2):
        spread(side)
    for q in range(5):
        rows_coefficients(q)
    for side in range(2):
        strips.faces(side, F, SK, SS0, DS, [16])
    for side in range(2):
        strips.coefficients(side, F, SK, DS, put_far(side), [16])
    for step in range(STEPS):
        now, later = (SS0, SS1) if step % 2 == 0 else (SS1, SS0)
        for side in range(2):
            strips.vertical(side, now, SK, U)
        for q in range(5 - step):
            rows_step(step, q)
        for side in range(2):
            strips.step(side, now, SK, SK2, U, DS)
        rows_update(step)
        for side in range(2):
            strips.update(side, later, DS)

    rows_last, strips_last = (SB, SS1) if STEPS % 2 else (SA, SS0)
    copies = []
    for side, t, rim in ((0, 0, sub < 3), (1, 15, sub >= 5)):
        edges = strips.edge(strips_last, spot[t])
        for c in range(2):
            for q in range(3):
                kk = level(q, lev)
                edge = roll(edges, 125 - 10 * (6 * c + q), 1)
                x = jnp.where((lane < 3) | (lane >= 125), edge, rows_last[c, q + 1, spot[t]])
                whole[side, c, kk] = jnp.where(rim, x, rims[side, c, kk])
        copy = pltpu.make_async_copy(whole.at[side], out.at[:, :, tile(t)], sem.at[side])
        copy.start()
        copies.append(copy)
    for copy in copies:
        copy.wait()


PREP_SCRATCH = [(2, 9, 128, 128), (2, 1, 128, 128)]
STRIP_SCRATCH = [
    (2, 128, 128), (2, 128, 128), (2, 128, 128), (2, 3, 128, 128), (2, 3, 128, 128),
    pltpu.SemaphoreType.DMA((6,)),
]
FRAME_SCRATCH = [
    (2, 7, 24, 128), (2, 7, 24, 128), (7, 24, 128), (5, 9, 24, 128), (5, 4, 8, 128), (5, 2, 3, 24, 128),
    (2, 9, 24, 128), (2, 9, 24, 128), (2, 4, 8, 128), (2, 24, 128), (2, 24, 128), (2, 24, 128), (2, 3, 24, 128),
    (2, 2, 3, 8, 128), pltpu.SemaphoreType.DMA((2,)),
]


def call(kernel, shapes, scratch=(), types=(), in_specs=None, out_specs=None, aliases=None, cost=None):
    types = list(types) + [f32] * (len(shapes) - len(types))
    return pl.pallas_call(
        kernel,
        out_shape=[jax.ShapeDtypeStruct(s, d) for s, d in zip(shapes, types)],
        **({} if in_specs is None else dict(in_specs=in_specs)),
        out_specs=out_specs or [VMEM] * len(shapes),
        scratch_shapes=[pltpu.VMEM(s, f32) if isinstance(s, tuple) else s for s in scratch],
        compiler_params=PARAMS,
        input_output_aliases=aliases or {},
        cost_estimate=cost and pl.CostEstimate(flops=cost, bytes_accessed=cost, transcendentals=0),
    )


def local(tracers, land_sea, faces_east, faces_north):
    lons, lats = lax.axis_size("lon"), lax.axis_size("lat")
    swap = [(0, 1), (1, 0)]

    inputs = (tracers, land_sea, faces_east, faces_north)
    hbm = pl.BlockSpec(memory_space=pltpu.HBM)
    *blocks, to_east, to_west = call(
        edges_kernel,
        [x.shape for x in inputs] + [(128, 128), (128, 128)],
        [(3, 128, 128), pltpu.SemaphoreType.DMA((9,))],
        types=[x.dtype for x in inputs],
        in_specs=[hbm] * 4,
    )(*[pltpu.with_memory_space_constraint(x, pltpu.HBM) for x in inputs])
    from_west = lax.ppermute(to_east, "lon", [(i, (i + 1) % lons) for i in range(lons)])
    from_east = lax.ppermute(to_west, "lon", [((i + 1) % lons, i) for i in range(lons)])
    levels, rows_a, rows_b = call(planes_kernel, [(21, 128, 128), (17, 8, 128), (17, 8, 128)])(*blocks)
    lev_in = lax.ppermute(levels, "lev", swap)
    block, strip, block_ends = call(
        block_kernel,
        [(2, 3, 128, 128), (2, 3, 128, 128), (5, 9, 2, 8, 128)],
        [(2, 7, 128, 128), (2, 7, 128, 128), (7, 128, 128), (5, 9, 128, 128), (2, 3, 128, 128)],
        cost=20_000_000,
    )(*blocks, lev_in)
    full, rows_a, rows_b = call(rows_kernel, [(2, 3, 128, 128), (17, 8, 128), (17, 8, 128)])(
        strip, from_east, from_west, rows_a, rows_b
    )

    def at(lon, lat):
        return lon * lats + lat

    route_a, route_b = [], []
    for lon in range(lons):
        for lat in range(lats):
            other = lat + 1 if lat % 2 == 0 else lat - 1
            route_a.append((at(lon, lat), at(lon, other)))
            if lat == lats - 1:
                route_b.append((at(lon, lat), at(lons - 1 - lon, lat)))
            elif lat > 0:
                other = lat - 1 if lat % 2 == 0 else lat + 1
                route_b.append((at(lon, lat), at(lon, other)))
    got_a = lax.ppermute(rows_a, ("lon", "lat"), route_a)
    got_b = lax.ppermute(rows_b, ("lon", "lat"), route_b)
    full_p = lax.ppermute(full, "lev", swap)
    coefs, first, strip_ends = call(
        strip_prep_kernel,
        [(2, 9, 128, 128), (2, 128, 128), (2, 9, 2, 8, 128)],
        PREP_SCRATCH,
        cost=4_000_000,
    )(full, full_p)
    (both,) = call(stack_kernel, [(2, 17, 8, 128)])(got_a, got_b, first)
    both_p = lax.ppermute(both, "lev", swap)
    out, rims = call(
        strip_steps_kernel,
        [(2, 3, 128, 128), (2, 2, 3, 8, 128)],
        STRIP_SCRATCH,
        out_specs=[hbm, VMEM],
        cost=6_000_000,
    )(coefs, first, block, both)
    (out,) = call(
        frame_kernel,
        [(2, 3, 128, 128)],
        FRAME_SCRATCH,
        in_specs=[VMEM] * 11 + [hbm],
        out_specs=[hbm],
        aliases={11: 0},
    )(*blocks, lev_in, rims, block_ends, strip_ends, coefs, both, both_p, out)
    return out


def solution(mesh):
    return jax.shard_map(
        local,
        mesh=mesh,
        in_specs=(
            P("members", "lev", "lat", "lon"),
            P("lev", "lat", "lon"),
            P("members", "lev", "lat", "lon"),
            P("members", "lev", "lat", "lon"),
        ),
        out_specs=P("members", "lev", "lat", "lon"),
        check_vma=False,
    )
```

```python
import jax
import jax.numpy as jnp
from jax import lax
from jax.experimental import pallas as pl
from jax.experimental.pallas import tpu as pltpu
from jax.sharding import PartitionSpec as P

STEPS = 3
S0, EV, S1, ED, ES, NV, ND, NS, WET = range(9)
R = 136
VMEM = pl.BlockSpec(memory_space=pltpu.VMEM)
PARAMS = pltpu.CompilerParams(vmem_limit_bytes=40 * 2**20)
f32 = jnp.float32


def iota(shape, dim):
    return lax.broadcasted_iota(jnp.int32, shape, dim)


def roll(x, shift, axis):
    shift %= x.shape[axis]
    return x if shift == 0 else pltpu.roll(x, shift, axis)


def position():
    lev = lax.axis_index("lev")
    lat = lax.axis_index("lat")
    odd = lax.rem(lat, 2) == 1
    last = lat == lax.axis_size("lat") - 1
    return lev, odd, last


def level(q, lev):
    return q + lev * (2 - 2 * q)


def raw(refs, n, kk, rows):
    tr, ls, fe, fn = refs
    if n == WET:
        return ls[kk, rows].astype(f32)
    if n in (S0, S1):
        return tr[n // 2, kk, rows]
    if n in (EV, ED, ES):
        return fe[(EV, ED, ES).index(n), kk, rows]
    return fn[n - NV, kk, rows]


def edges_kernel(tr, ls, fe, fn, tr_v, ls_v, fe_v, fn_v, east_ref, west_ref, edge_ref, sem):
    lev, _, _ = position()
    lane = iota((8, 128), 1)
    m = lane % 10
    sources, targets = (tr, ls, fe, fn), (tr_v, ls_v, fe_v, fn_v)
    copies = []
    for i in range(3):
        copies.append([])
        for n in range(4 * i, min(4 * i + 4, 9)):
            if n == WET:
                which, lead = 1, ()
            elif n in (S0, S1):
                which, lead = 0, (n // 2,)
            elif n in (EV, ED, ES):
                which, lead = 2, ((EV, ED, ES).index(n),)
            else:
                which, lead = 3, (n - NV,)
            source, target = sources[which], targets[which]
            if lead:
                source, target = source.at[lead[0]], target.at[lead[0]]
            copy = pltpu.make_async_copy(source, target, sem.at[n])
            copy.start()
            copies[i].append(copy)
    for i in range(3):
        for copy in copies[i]:
            copy.wait()
        for t in range(16):
            rows = pl.ds(8 * t, 8)
            packed = jnp.zeros((8, 128), f32)
            for n in range(4 * i, min(4 * i + 4, 9)):
                for q in range(3):
                    x = raw(targets, n, level(q, lev), rows)
                    at = 30 * (n % 4) + 10 * q + 3 * i
                    packed = jnp.where((lane >= at) & (lane < at + 6), roll(x, at - 125, 1), packed)
            edge_ref[i, rows] = packed
    for t in range(16):
        rows = pl.ds(8 * t, 8)
        a, b, c = edge_ref[0, rows], edge_ref[1, rows], edge_ref[2, rows]
        east_ref[rows] = jnp.where(m < 3, a, jnp.where(m < 6, b, c))
        west_ref[rows] = jnp.where((m >= 3) & (m < 6), a, jnp.where((m >= 6) & (m < 9), b, c))


def planes_kernel(tr, ls, fe, fn, lev_ref, a_ref, b_ref):
    refs = (tr, ls, fe, fn)
    lev, odd, last = position()
    lane = iota((8, 128), 1)
    sub = iota((8, 128), 0)
    for q in range(3):
        kk = level(q, lev)
        for c in range(2):
            lev_ref[3 * c + q] = tr[c, kk]
        lev_ref[6 + q] = ls[kk].astype(f32)
        if q >= 1:
            for face in range(3):
                lev_ref[9 + face * 2 + q - 1] = fe[face, kk]
                lev_ref[15 + face * 2 + q - 1] = fn[face, kk]

    def ends(p):
        if p >= 27:
            return (jnp.zeros((8, 128), f32),) * 2
        n, q = divmod(p, 3)
        kk = level(q, lev)
        return raw(refs, n, kk, pl.ds(120, 8)), raw(refs, n, kk, pl.ds(0, 8))

    for j in range(17):
        n, n2 = j // 3, (j + 17) // 3
        top, bottom = ends(j)
        top2, bottom2 = ends(j + 17)
        as_south = jnp.where(sub >= 4, top, roll(top2, 4, 0))
        as_north = jnp.where(sub < 4, bottom, roll(bottom2, 4, 0))
        folded = jnp.take_along_axis(jnp.take_along_axis(as_south, 7 - sub, axis=0), 127 - lane, axis=1)
        if n in (EV, ED, ES):
            folded = jnp.where(sub < 4, roll(folded, -1, 1), folded)
        if n in (EV, ES, NV, NS):
            folded = jnp.where(sub < 4, -folded, folded)
        if n2 in (NV, NS):
            folded = jnp.where(sub >= 4, -folded, folded)
        a_ref[j] = jnp.where(odd, as_north, as_south)
        b_ref[j] = jnp.where(odd, jnp.where(last, folded, as_south), as_north)


def rows_kernel(strip, from_east, from_west, a_in, b_in, full_ref, a_ref, b_ref):
    lev, odd, last = position()
    m = iota((128, 128), 1) % 10
    e, w = from_east[...], from_west[...]
    for i in range(3):
        full_ref[0, i] = jnp.where((m >= 6) & (m < 9), roll(e, 3 - 3 * i, 1), strip[0, i])
        full_ref[1, i] = jnp.where(m < 3, roll(w, -3 * i, 1), strip[1, i])
    lane = iota((8, 128), 1)
    sub = iota((8, 128), 0)
    m = lane % 10
    group = lane - m
    quarter = lane // 30
    for j in range(17):
        if not 10 <= j < 16:
            a_ref[j] = a_in[j]
            b_ref[j] = b_in[j]
    turned = []
    for j in range(10, 16):
        side, i = divmod(j - 10, 3)
        top, bottom = full_ref[side, i, pl.ds(120, 8)], full_ref[side, i, pl.ds(0, 8)]
        swapped = jnp.take_along_axis(full_ref[1 - side, i, pl.ds(120, 8)], 7 - sub, axis=0)
        if side == 0:
            turned.append(swapped)
        east_item = [(quarter == 1) | (quarter == 3), quarter == 0, quarter < 0][i]
        negative = [quarter == 1, (quarter == 0) | (quarter == 1) | (quarter == 3), quarter < 0][i]
        source = jnp.clip(group + jnp.where(east_item, 7, 8) - m, 0, 127)
        folded = jnp.take_along_axis(swapped, source, axis=1)
        folded = jnp.where(negative, -folded, folded)
        as_south, as_north, folded = roll(top, 4, 0), roll(bottom, 4, 0), roll(folded, 4, 0)
        a_ref[j] = jnp.where(
            odd, jnp.where(sub < 4, a_in[j], as_north), jnp.where(sub >= 4, a_in[j], as_south)
        )
        b_south = jnp.where(sub >= 4, b_in[j], as_south)
        b_north = jnp.where(sub < 4, b_in[j], jnp.where(last, folded, as_north))
        b_ref[j] = jnp.where(jnp.logical_and(odd, jnp.logical_not(last)), b_south, b_north)
    for n in (EV, ED, ES):
        for q in range(3):
            j = 3 * n + q
            at = 30 * (n % 4) + 10 * q + 2
            x = roll(turned[n // 4], 127 - at, 1)
            x = x if n == ED else -x
            b_ref[j] = jnp.where((lane == 127) & (sub < 4) & last, x, b_ref[j])


def coefficients(v, d, slope, wet):
    return (
        wet * (jnp.maximum(v, 0.0) + d),
        wet * (jnp.minimum(v, 0.0) - d),
        wet * (d * 0.25 * slope),
    )


def tile(t):
    return pl.ds(8 * t, 8)


def rows_up(sub, here, above):
    return jnp.where(sub == 7, roll(above, -1, 0), roll(here, -1, 0))


def rows_down(sub, here, below):
    return jnp.where(sub == 0, roll(below, 1, 0), roll(here, 1, 0))


def north_coefficients(ring, v, d, s, wet, put, far=None):
    sub = iota((8, 128), 0)
    size = len(ring)
    known = {}
    for at in [size - 1] + list(range(size)):
        t = ring[at]
        if t not in known:
            wet_t = wet(t) * rows_up(sub, wet(t), wet(ring[(at + 1) % size]))
            known[t] = coefficients(v(t), d(t), s(t), wet_t)
            if far and t == 15:
                x, y, z = coefficients(*(roll(f, -1, 0) for f in far[:3]), wet_t)
                beyond = jnp.logical_and(far[3], sub == 7)
                a2, b2, c2 = (jnp.where(beyond, f, g) for f, g in zip((x, y, z), known[t]))
                far[4](0, a2)
                far[4](1, c2)
        below = known.get(ring[at - 1])
        if below is not None:
            a, b, c = known[t]
            put(t, 4, a)
            put(t, 5, c)
            put(t, 6, rows_down(sub, b, below[1]))
            put(t, 7, rows_down(sub, c, below[2]))
            if far and t == 16:
                far[4](2, rows_down(sub, b, b2))
                far[4](3, rows_down(sub, c, c2))


def terms(ring, coef, coef2, state, vertical, push, skip=()):
    sub = iota((8, 128), 0)
    size = len(ring)
    held = {}

    def make(t):
        s, u = state(t), vertical(t)
        up_face = coef(t, 4) * s + coef(t, 5) * u
        down_face = coef(t, 6) * s + coef(t, 7) * u
        far, near = up_face, down_face
        if coef2 and t == 15:
            far = coef2(0) * s + coef2(1) * u
        if coef2 and t == 16:
            near = coef2(2) * s + coef2(3) * u
        part = None
        if t not in skip:
            east, west = coef(t, 0) * s + coef(t, 1) * u, coef(t, 2) * s + coef(t, 3) * u
            push(t, east, west)
            part = s + (west - east) + (near - up_face)
        held[t] = part, up_face, far, down_face

    make(ring[-1])
    make(ring[0])
    for at, t in enumerate(ring):
        if at + 1 < size - 1:
            make(ring[at + 1])
        if t in skip:
            continue
        part, up_face, _, down_face = held[t]
        x = rows_down(sub, up_face, held[ring[at - 1]][2])
        y = rows_up(sub, down_face, held[ring[(at + 1) % size]][3])
        yield t, part + (x - y)


def block_kernel(tr, ls, fe, fn, lev_in, out, strip_ref, ends, SA, SB, W, K, D):
    lev, _, _ = position()
    refs = (tr, ls, fe, fn)
    lane = iota((8, 128), 1)
    ring = list(range(16))
    half = jnp.where(lev == 0, 0.5, -0.5)
    zero = jnp.zeros((128, 128), f32)

    for t in ring:
        for i in range(3):
            east = west = jnp.zeros((8, 128), f32)
            for n in range(4 * i, min(4 * i + 4, 9)):
                for q in range(3):
                    x = raw(refs, n, level(q, lev), tile(t))
                    at = 30 * (n % 4) + 10 * q
                    east = jnp.where((lane >= at) & (lane < at + 6), roll(x, at - 122, 1), east)
                    west = jnp.where((lane >= at + 3) & (lane < at + 9), roll(x, at + 3, 1), west)
            strip_ref[0, i, tile(t)] = east
            strip_ref[1, i, tile(t)] = west

    for c in range(2):
        SA[c, 0] = zero
        SB[c, 0] = zero
    W[0] = zero
    for q in range(3):
        kk = level(q, lev)
        for c in range(2):
            SA[c, q + 1] = tr[c, kk]
            SA[c, 6 - q] = lev_in[3 * c + q]
        W[q + 1] = ls[kk].astype(f32)
        W[6 - q] = lev_in[6 + q]

    for q in range(5):
        kk = level(min(q, 2), lev)

        def field(n, t):
            if q >= 3:
                return lev_in[9 + (EV, ED, ES, NV, ND, NS).index(n) * 2 + 4 - q, tile(t)]
            return raw(refs, n, kk, tile(t))

        for t in ring:
            wet = W[q + 1, tile(t)]
            D[0, 0, tile(t)] = wet * roll(wet, -1, 1)
            K[q, 8, tile(t)] = half * W[q, tile(t)] * wet * W[q + 2, tile(t)]
        for t in ring:
            a, b, c = coefficients(field(EV, t), field(ED, t), field(ES, t), D[0, 0, tile(t)])
            K[q, 0, tile(t)] = a
            K[q, 1, tile(t)] = c
            K[q, 2, tile(t)] = roll(b, 1, 1)
            K[q, 3, tile(t)] = roll(c, 1, 1)

        def put(t, at, x):
            K[q, at, tile(t)] = x

        north_coefficients(
            ring, lambda t: field(NV, t), lambda t: field(ND, t), lambda t: field(NS, t),
            lambda t: W[q + 1, tile(t)], put,
        )
        for k in (0, 1, 2, 3, 8):
            ends[q, k, 0] = K[q, k, tile(0)]
            ends[q, k, 1] = K[q, k, tile(15)]

    for step in range(STEPS):
        now, later = (SA, SB) if step % 2 == 0 else (SB, SA)

        @pl.loop(0, 5 - step)
        def _(q):
            for c in range(2):
                def push(t, east, west):
                    D[c, 0, tile(t)] = roll(east, 1, 1)
                    D[c, 1, tile(t)] = roll(west, -1, 1)

                def vertical(t):
                    return K[q, 8, tile(t)] * (now[c, q + 2, tile(t)] - now[c, q, tile(t)])

                for t, part in terms(
                    ring, lambda t, i: K[q, i, tile(t)], None,
                    lambda t: now[c, q + 1, tile(t)], vertical, push,
                ):
                    D[c, 2, tile(t)] = part
            for c in range(2):
                for t in ring:
                    x = D[c, 2, tile(t)] + (D[c, 0, tile(t)] - D[c, 1, tile(t)])
                    if step == STEPS - 1:
                        out[c, level(q, lev), tile(t)] = x
                    else:
                        later[c, q + 1, tile(t)] = x


class Strips:
    def __init__(self, ring, spot, lev):
        self.ring, self.spot = ring, spot
        self.half = jnp.where(lev == 0, 0.5, -0.5)
        lane = iota((8, 128), 1)
        m = lane % 10
        group = lane // 10
        self.second = group >= 6
        self.q = group % 6
        self.mine = self.q < 3
        self.used = (lane < 120) & (m < 9)
        self.index = jnp.where(self.mine, 10 * self.q + m, 10 * (5 - self.q) + m)

    def pick(self, n, own, partner):
        index = self.index + (jnp.where(self.second, 60, 0) if n == S0 else 30 * (n % 4))
        index = jnp.clip(index, 0, 127)
        x = jnp.take_along_axis(own, index, axis=1)
        y = jnp.take_along_axis(partner, index, axis=1)
        return jnp.where(self.used, jnp.where(self.mine, x, y), 0.0)

    def faces(self, side, F, SK, first, D, tiles=None):
        outside = (self.q == 0) | (self.q == 5)
        for t in tiles or self.ring:
            at = self.spot[t]
            wet = F[side, WET, at]
            D[side, 0, at] = wet * roll(wet, -1, 1)
            around = roll(wet, -10, 1) * roll(wet, 10, 1)
            SK[side, 8, at] = jnp.where(outside, 0.0, self.half * wet * around)
            first[side, at] = F[side, S0, at]

    def coefficients(self, side, F, SK, D, far=None, tiles=None):
        for t in tiles or self.ring:
            at = self.spot[t]
            a, b, c = coefficients(*(F[side, n, at] for n in (EV, ED, ES)), D[side, 0, at])
            SK[side, 0, at] = a
            SK[side, 1, at] = c
            SK[side, 2, at] = roll(b, 1, 1)
            SK[side, 3, at] = roll(c, 1, 1)

        def put(t, k, x):
            SK[side, k, self.spot[t]] = x

        north_coefficients(
            self.ring, *(lambda t, n=n: F[side, n, self.spot[t]] for n in (NV, ND, NS, WET)), put, far
        )

    def vertical(self, side, now, SK, U):
        for t in self.ring:
            at = self.spot[t]
            s = now[side, at]
            U[side, at] = SK[side, 8, at] * (roll(s, -10, 1) - roll(s, 10, 1))

    def step(self, side, now, SK, SK2, U, D):
        def push(t, east, west):
            D[side, 0, self.spot[t]] = roll(east, 1, 1)
            D[side, 1, self.spot[t]] = roll(west, -1, 1)

        for t, part in terms(
            self.ring, lambda t, k: SK[side, k, self.spot[t]],
            None if SK2 is None else lambda k: SK2[side, k],
            lambda t: now[side, self.spot[t]], lambda t: U[side, self.spot[t]], push,
        ):
            D[side, 2, self.spot[t]] = part

    def update(self, side, later, D):
        for t in self.ring:
            at = self.spot[t]
            later[side, at] = D[side, 2, at] + (D[side, 0, at] - D[side, 1, at])

    def edge(self, last_strips, at):
        m = iota((8, 128), 1) % 10
        return jnp.where(m < 3, roll(last_strips[0, at], -3, 1), last_strips[1, at])


def strip_prep_kernel(strip_o, strip_p, SK, first, ends, F, D):
    lev, _, _ = position()
    strips = Strips(list(range(16)), {t: tile(t) for t in range(16)}, lev)
    for side in range(2):
        for n in range(9):
            if n != S1:
                for t in range(16):
                    F[side, n, tile(t)] = strips.pick(
                        n, strip_o[side, n // 4, tile(t)], strip_p[side, n // 4, tile(t)]
                    )
    for side in range(2):
        strips.faces(side, F, SK, first, D)
    for side in range(2):
        strips.coefficients(side, F, SK, D)
    for side in range(2):
        for n in range(9):
            if n != S1:
                ends[side, n, 0] = F[side, n, tile(0)]
                ends[side, n, 1] = F[side, n, tile(15)]


def stack_kernel(a, b, _, both):
    both[0] = a[...]
    both[1] = b[...]


def strip_steps_kernel(SK, first, block, _, whole, SA, SB, U, D):
    lev, _, _ = position()
    lane = iota((8, 128), 1)
    strips = Strips(list(range(16)), {t: tile(t) for t in range(16)}, lev)
    now = first
    for step in range(STEPS):
        later = SB if step % 2 else SA
        for side in range(2):
            strips.vertical(side, now, SK, U)
        for side in range(2):
            strips.step(side, now, SK, None, U, D)
        for side in range(2):
            strips.update(side, later, D)
        now = later
    for t in range(16):
        U[0, tile(t)] = strips.edge(now, tile(t))
    for c in range(2):
        for q in range(3):
            kk = level(q, lev)
            for t in range(16):
                edge = roll(U[0, tile(t)], 125 - 10 * (6 * c + q), 1)
                whole[c, kk, tile(t)] = jnp.where((lane < 3) | (lane >= 125), edge, block[c, kk, tile(t)])


def frame_kernel(
    tr, ls, fe, fn, lev_in, most, block_ends, strip_ends, strip_coefs, rows_o, rows_p,
    out, SA, SB, W, K, K2, D, F, SK, SK2, SS0, SS1, U, DS, rims, sem,
):
    lev, odd, last = position()
    refs = (tr, ls, fe, fn)
    lane = iota((8, 128), 1)
    sub = iota((8, 128), 0)
    half = jnp.where(lev == 0, 0.5, -0.5)
    ring = [15, 16, 0]
    spot = {15: pl.ds(0, 8), 16: pl.ds(8, 8), 0: pl.ds(16, 8)}

    def halo(p, partner):
        rows = rows_p if partner else rows_o
        x, y = rows[0, p % 17], rows[1, p % 17]
        north, south = jnp.where(odd, y, x), jnp.where(odd, x, y)
        if p >= 17:
            north, south = roll(north, 4, 0), roll(south, 4, 0)
        return north, jnp.where(sub >= 5, south, 0.0)

    def joined(n, north, south):
        if n in (NV, ND, NS):
            return jnp.where(sub < 2, jnp.where(last, roll(north, -1, 0), north), south)
        return jnp.where(sub < 3, north, south)

    middle = pl.ds(8, 112)
    bulk = pltpu.make_async_copy(most.at[:, :, middle], out.at[:, :, middle], sem.at[2])
    bulk.start()

    zero = jnp.zeros((24, 128), f32)
    for c in range(2):
        SA[c, 0] = zero
        SB[c, 0] = zero
    W[0] = zero
    for q in range(3):
        kk = level(q, lev)
        for t in (15, 0):
            for c in range(2):
                SA[c, q + 1, spot[t]] = tr[c, kk, tile(t)]
                SA[c, 6 - q, spot[t]] = lev_in[3 * c + q, tile(t)]
            W[q + 1, spot[t]] = ls[kk, tile(t)].astype(f32)
            W[6 - q, spot[t]] = lev_in[6 + q, tile(t)]
        for c in range(2):
            SA[c, q + 1, spot[16]] = joined(S0, *halo(3 * (S0, S1)[c] + q, False))
            SA[c, 6 - q, spot[16]] = joined(S0, *halo(3 * (S0, S1)[c] + q, True))
        W[q + 1, spot[16]] = joined(WET, *halo(3 * WET + q, False))
        W[6 - q, spot[16]] = joined(WET, *halo(3 * WET + q, True))

    def rows_coefficients(q):
        partner = q >= 3
        qq = 5 - q if partner else q
        kk = level(qq, lev)

        def field(n, t):
            if t == 16:
                return joined(n, *halo(3 * n + qq, partner))
            if partner:
                return lev_in[9 + (EV, ED, ES, NV, ND, NS).index(n) * 2 + qq - 1, tile(t)]
            return raw(refs, n, kk, tile(t))

        for k in (0, 1, 2, 3, 8):
            K[q, k, spot[0]] = block_ends[q, k, 0]
            K[q, k, spot[15]] = block_ends[q, k, 1]
        a, b, c = coefficients(field(EV, 16), field(ED, 16), field(ES, 16), D[q, 0, 0, spot[16]])
        K[q, 0, spot[16]] = a
        K[q, 1, spot[16]] = c
        K[q, 2, spot[16]] = roll(b, 1, 1)
        K[q, 3, spot[16]] = roll(c, 1, 1)
        K[q, 8, spot[16]] = half * W[q, spot[16]] * W[q + 1, spot[16]] * W[q + 2, spot[16]]

        def put(t, at, x):
            K[q, at, spot[t]] = x

        def put2(at, x):
            K2[q, at] = x

        north_coefficients(
            ring, lambda t: field(NV, t), lambda t: field(ND, t), lambda t: field(NS, t),
            lambda t: W[q + 1, spot[t]], put,
            (*(halo(3 * n + qq, partner)[0] for n in (NV, ND, NS)), last, put2),
        )

    def rows_step(step, q):
        now = SA if step % 2 == 0 else SB
        for c in range(2):
            def push(t, east, west):
                D[q, c, 0, spot[t]] = roll(east, 1, 1)
                D[q, c, 1, spot[t]] = roll(west, -1, 1)

            def vertical(t):
                return K[q, 8, spot[t]] * (now[c, q + 2, spot[t]] - now[c, q, spot[t]])

            for t, part in terms(
                ring, lambda t, i: K[q, i, spot[t]], lambda i: K2[q, i],
                lambda t: now[c, q + 1, spot[t]], vertical, push,
            ):
                D[q, c, 2, spot[t]] = part

    def rows_update(step):
        later = SB if step % 2 == 0 else SA
        for q in range(5 - step):
            for c in range(2):
                later[c, q + 1] = D[q, c, 2] + (D[q, c, 0] - D[q, c, 1])

    strips = Strips(ring, spot, lev)
    far = [[None] * 3, [None] * 3]

    def spread(side):
        for n in range(9):
            if n == S1:
                continue
            i = n // 4
            F[side, n, spot[0]] = strip_ends[side, n, 0]
            F[side, n, spot[15]] = strip_ends[side, n, 1]
            p = 27 + 3 * side + i
            north, south = (strips.pick(n, x, y) for x, y in zip(halo(p, False), halo(p, True)))
            F[side, n, spot[16]] = joined(n, north, south)
            if n in (NV, ND, NS):
                far[side][n - NV] = north
        for t in (0, 15):
            SS0[side, spot[t]] = F[side, S0, spot[t]]
            for k in (0, 1, 2, 3, 8):
                SK[side, k, spot[t]] = strip_coefs[side, k, tile(t)]

    def put_far(side):
        def put(k, x):
            SK2[side, k] = x
        return (*far[side], last, put)

    for q in range(5):
        wet = W[q + 1, spot[16]]
        D[q, 0, 0, spot[16]] = wet * roll(wet, -1, 1)
    for side in range(2):
        spread(side)
    for q in range(5):
        rows_coefficients(q)
    for side in range(2):
        strips.faces(side, F, SK, SS0, DS, [16])
    for side in range(2):
        strips.coefficients(side, F, SK, DS, put_far(side), [16])
    for step in range(STEPS):
        now, later = (SS0, SS1) if step % 2 == 0 else (SS1, SS0)
        for side in range(2):
            strips.vertical(side, now, SK, U)
        for q in range(5 - step):
            rows_step(step, q)
        for side in range(2):
            strips.step(side, now, SK, SK2, U, DS)
        rows_update(step)
        for side in range(2):
            strips.update(side, later, DS)

    rows_last, strips_last = (SB, SS1) if STEPS % 2 else (SA, SS0)
    copies = [bulk]
    for side, t, rim in ((0, 0, sub < 3), (1, 15, sub >= 5)):
        edges = strips.edge(strips_last, spot[t])
        for c in range(2):
            for q in range(3):
                kk = level(q, lev)
                edge = roll(edges, 125 - 10 * (6 * c + q), 1)
                x = jnp.where((lane < 3) | (lane >= 125), edge, rows_last[c, q + 1, spot[t]])
                rims[side, c, kk] = jnp.where(rim, x, most[c, kk, tile(t)])
        copy = pltpu.make_async_copy(rims.at[side], out.at[:, :, tile(t)], sem.at[side])
        copy.start()
        copies.append(copy)
    for copy in copies:
        copy.wait()


PREP_SCRATCH = [(2, 9, 128, 128), (2, 1, 128, 128)]
STRIP_SCRATCH = [(2, 128, 128), (2, 128, 128), (2, 128, 128), (2, 3, 128, 128)]
FRAME_SCRATCH = [
    (2, 7, 24, 128), (2, 7, 24, 128), (7, 24, 128), (5, 9, 24, 128), (5, 4, 8, 128), (5, 2, 3, 24, 128),
    (2, 9, 24, 128), (2, 9, 24, 128), (2, 4, 8, 128), (2, 24, 128), (2, 24, 128), (2, 24, 128), (2, 3, 24, 128),
    (2, 2, 3, 8, 128), pltpu.SemaphoreType.DMA((3,)),
]


def call(kernel, shapes, scratch=(), types=(), in_specs=None, out_specs=None, cost=None):
    types = list(types) + [f32] * (len(shapes) - len(types))
    return pl.pallas_call(
        kernel,
        out_shape=[jax.ShapeDtypeStruct(s, d) for s, d in zip(shapes, types)],
        **({} if in_specs is None else dict(in_specs=in_specs)),
        out_specs=out_specs or [VMEM] * len(shapes),
        scratch_shapes=[pltpu.VMEM(s, f32) if isinstance(s, tuple) else s for s in scratch],
        compiler_params=PARAMS,
        cost_estimate=cost and pl.CostEstimate(flops=cost, bytes_accessed=cost, transcendentals=0),
    )


def local(tracers, land_sea, faces_east, faces_north):
    lons, lats = lax.axis_size("lon"), lax.axis_size("lat")
    swap = [(0, 1), (1, 0)]

    inputs = (tracers, land_sea, faces_east, faces_north)
    hbm = pl.BlockSpec(memory_space=pltpu.HBM)
    *blocks, to_east, to_west = call(
        edges_kernel,
        [x.shape for x in inputs] + [(128, 128), (128, 128)],
        [(3, 128, 128), pltpu.SemaphoreType.DMA((9,))],
        types=[x.dtype for x in inputs],
        in_specs=[hbm] * 4,
    )(*[pltpu.with_memory_space_constraint(x, pltpu.HBM) for x in inputs])
    from_west = lax.ppermute(to_east, "lon", [(i, (i + 1) % lons) for i in range(lons)])
    from_east = lax.ppermute(to_west, "lon", [((i + 1) % lons, i) for i in range(lons)])
    levels, rows_a, rows_b = call(planes_kernel, [(21, 128, 128), (17, 8, 128), (17, 8, 128)])(*blocks)
    lev_in = lax.ppermute(levels, "lev", swap)
    block, strip, block_ends = call(
        block_kernel,
        [(2, 3, 128, 128), (2, 3, 128, 128), (5, 9, 2, 8, 128)],
        [(2, 7, 128, 128), (2, 7, 128, 128), (7, 128, 128), (5, 9, 128, 128), (2, 3, 128, 128)],
        cost=20_000_000,
    )(*blocks, lev_in)
    full, rows_a, rows_b = call(rows_kernel, [(2, 3, 128, 128), (17, 8, 128), (17, 8, 128)])(
        strip, from_east, from_west, rows_a, rows_b
    )

    def at(lon, lat):
        return lon * lats + lat

    route_a, route_b = [], []
    for lon in range(lons):
        for lat in range(lats):
            other = lat + 1 if lat % 2 == 0 else lat - 1
            route_a.append((at(lon, lat), at(lon, other)))
            if lat == lats - 1:
                route_b.append((at(lon, lat), at(lons - 1 - lon, lat)))
            elif lat > 0:
                other = lat - 1 if lat % 2 == 0 else lat + 1
                route_b.append((at(lon, lat), at(lon, other)))
    got_a = lax.ppermute(rows_a, ("lon", "lat"), route_a)
    got_b = lax.ppermute(rows_b, ("lon", "lat"), route_b)
    full_p = lax.ppermute(full, "lev", swap)
    coefs, first, strip_ends = call(
        strip_prep_kernel,
        [(2, 9, 128, 128), (2, 128, 128), (2, 9, 2, 8, 128)],
        PREP_SCRATCH,
        cost=4_000_000,
    )(full, full_p)
    (both,) = call(stack_kernel, [(2, 17, 8, 128)])(got_a, got_b, first)
    both_p = lax.ppermute(both, "lev", swap)
    (most,) = call(strip_steps_kernel, [(2, 3, 128, 128)], STRIP_SCRATCH, cost=6_000_000)(
        coefs, first, block, both
    )
    (out,) = call(frame_kernel, [(2, 3, 128, 128)], FRAME_SCRATCH, out_specs=[hbm])(
        *blocks, lev_in, most, block_ends, strip_ends, coefs, both, both_p
    )
    return out


def solution(mesh):
    return jax.shard_map(
        local,
        mesh=mesh,
        in_specs=(
            P("members", "lev", "lat", "lon"),
            P("lev", "lat", "lon"),
            P("members", "lev", "lat", "lon"),
            P("members", "lev", "lat", "lon"),
        ),
        out_specs=P("members", "lev", "lat", "lon"),
        check_vma=False,
    )
```

```python
import jax
import jax.numpy as jnp
from jax import lax
from jax.experimental import pallas as pl
from jax.experimental.pallas import tpu as pltpu
from jax.sharding import PartitionSpec as P

STEPS = 3
S0, EV, S1, ED, ES, NV, ND, NS, WET = range(9)
R = 136
VMEM = pl.BlockSpec(memory_space=pltpu.VMEM)
PARAMS = pltpu.CompilerParams(vmem_limit_bytes=40 * 2**20)
f32 = jnp.float32
TALL = [p for p in range(33) if p // 3 not in (EV, ED, ES)]
SHORT = [p for p in range(27) if p // 3 in (EV, ED, ES)]


def iota(shape, dim):
    return lax.broadcasted_iota(jnp.int32, shape, dim)


def roll(x, shift, axis):
    shift %= x.shape[axis]
    return x if shift == 0 else pltpu.roll(x, shift, axis)


def position():
    lev = lax.axis_index("lev")
    lat = lax.axis_index("lat")
    odd = lax.rem(lat, 2) == 1
    last = lat == lax.axis_size("lat") - 1
    return lev, odd, last


def level(q, lev):
    return q + lev * (2 - 2 * q)


def raw(refs, n, kk, rows):
    tr, ls, fe, fn = refs
    if n == WET:
        return ls[kk, rows].astype(f32)
    if n in (S0, S1):
        return tr[n // 2, kk, rows]
    if n in (EV, ED, ES):
        return fe[(EV, ED, ES).index(n), kk, rows]
    return fn[n - NV, kk, rows]


def edges_kernel(tr, ls, fe, fn, tr_v, ls_v, fe_v, fn_v, east_ref, west_ref, edge_ref, sem):
    lev, _, _ = position()
    lane = iota((8, 128), 1)
    m = lane % 10
    sources, targets = (tr, ls, fe, fn), (tr_v, ls_v, fe_v, fn_v)
    copies = []
    for i in range(3):
        copies.append([])
        for n in range(4 * i, min(4 * i + 4, 9)):
            if n == WET:
                which, lead = 1, ()
            elif n in (S0, S1):
                which, lead = 0, (n // 2,)
            elif n in (EV, ED, ES):
                which, lead = 2, ((EV, ED, ES).index(n),)
            else:
                which, lead = 3, (n - NV,)
            source, target = sources[which], targets[which]
            if lead:
                source, target = source.at[lead[0]], target.at[lead[0]]
            copy = pltpu.make_async_copy(source, target, sem.at[n])
            copy.start()
            copies[i].append(copy)
    for i in range(3):
        for copy in copies[i]:
            copy.wait()
        for t in range(16):
            rows = pl.ds(8 * t, 8)
            packed = jnp.zeros((8, 128), f32)
            for n in range(4 * i, min(4 * i + 4, 9)):
                for q in range(3):
                    x = raw(targets, n, level(q, lev), rows)
                    at = 30 * (n % 4) + 10 * q + 3 * i
                    packed = jnp.where((lane >= at) & (lane < at + 6), roll(x, at - 125, 1), packed)
            edge_ref[i, rows] = packed
    for t in range(16):
        rows = pl.ds(8 * t, 8)
        a, b, c = edge_ref[0, rows], edge_ref[1, rows], edge_ref[2, rows]
        east_ref[rows] = jnp.where(m < 3, a, jnp.where(m < 6, b, c))
        west_ref[rows] = jnp.where((m >= 3) & (m < 6), a, jnp.where((m >= 6) & (m < 9), b, c))


def planes_kernel(tr, ls, fe, fn, lev_ref, a_ref, b_ref):
    refs = (tr, ls, fe, fn)
    lev, odd, last = position()
    lane = iota((8, 128), 1)
    sub = iota((8, 128), 0)
    for q in range(3):
        kk = level(q, lev)
        for c in range(2):
            lev_ref[3 * c + q] = tr[c, kk]
        lev_ref[6 + q] = ls[kk].astype(f32)
        if q >= 1:
            for face in range(3):
                lev_ref[9 + face * 2 + q - 1] = fe[face, kk]
                lev_ref[15 + face * 2 + q - 1] = fn[face, kk]

    def ends(p):
        if p >= 27:
            return (jnp.zeros((8, 128), f32),) * 2
        n, q = divmod(p, 3)
        kk = level(q, lev)
        return raw(refs, n, kk, pl.ds(120, 8)), raw(refs, n, kk, pl.ds(0, 8))

    none = (jnp.zeros((8, 128), f32),) * 2
    for j in range(12):
        (top, bottom), (top2, bottom2) = ends(TALL[j]), ends(TALL[j + 12])
        top3, bottom3 = ends(SHORT[j]) if j < 9 else none
        as_south = jnp.where(sub >= 5, top, jnp.where(sub >= 2, roll(top2, -3, 0), roll(top3, 2, 0)))
        as_north = jnp.where(sub < 3, bottom, jnp.where(sub < 6, roll(bottom2, 3, 0), roll(bottom3, 6, 0)))
        folded = jnp.take_along_axis(jnp.take_along_axis(as_south, 7 - sub, axis=0), 127 - lane, axis=1)
        folded = jnp.where(sub >= 6, roll(folded, -1, 1), folded)
        if TALL[j] // 3 in (NV, NS):
            folded = jnp.where(sub < 3, -folded, folded)
        if TALL[j + 12] // 3 in (NV, NS):
            folded = jnp.where((sub >= 3) & (sub < 6), -folded, folded)
        if j < 9 and SHORT[j] // 3 in (EV, ES):
            folded = jnp.where(sub >= 6, -folded, folded)
        a_ref[j] = jnp.where(odd, as_north, as_south)
        b_ref[j] = jnp.where(odd, jnp.where(last, folded, as_south), as_north)


def rows_kernel(strip, from_east, from_west, a_in, b_in, b_ref, a_ref, full_ref):
    lev, odd, last = position()
    m = iota((128, 128), 1) % 10
    e, w = from_east[...], from_west[...]
    for i in range(3):
        full_ref[0, i] = jnp.where((m >= 6) & (m < 9), roll(e, 3 - 3 * i, 1), strip[0, i])
        full_ref[1, i] = jnp.where(m < 3, roll(w, -3 * i, 1), strip[1, i])
    lane = iota((8, 128), 1)
    sub = iota((8, 128), 0)
    m = lane % 10
    group = lane - m
    quarter = lane // 30
    for j in range(6):
        a_ref[j] = a_in[j]
        b_ref[j] = b_in[j]
    south_spot, north_spot = (sub >= 2) & (sub < 5), (sub >= 3) & (sub < 6)
    turned = []
    for j in range(6, 12):
        side, i = divmod(j - 6, 3)
        top, bottom = full_ref[side, i, pl.ds(120, 8)], full_ref[side, i, pl.ds(0, 8)]
        swapped = jnp.take_along_axis(full_ref[1 - side, i, pl.ds(120, 8)], 7 - sub, axis=0)
        if side == 0:
            turned.append(swapped)
        east_item = [(quarter == 1) | (quarter == 3), quarter == 0, quarter < 0][i]
        negative = [quarter == 1, (quarter == 0) | (quarter == 1) | (quarter == 3), quarter < 0][i]
        source = jnp.clip(group + jnp.where(east_item, 7, 8) - m, 0, 127)
        folded = jnp.take_along_axis(swapped, source, axis=1)
        folded = jnp.where(negative, -folded, folded)
        as_south, as_north, folded = roll(top, -3, 0), roll(bottom, 3, 0), roll(folded, 3, 0)
        a_ref[j] = jnp.where(
            odd, jnp.where(north_spot, as_north, a_in[j]), jnp.where(south_spot, as_south, a_in[j])
        )
        b_south = jnp.where(south_spot, as_south, b_in[j])
        b_north = jnp.where(north_spot, jnp.where(last, folded, as_north), b_in[j])
        b_ref[j] = jnp.where(jnp.logical_and(odd, jnp.logical_not(last)), b_south, b_north)
    for n in (EV, ED, ES):
        for q in range(3):
            j = SHORT.index(3 * n + q)
            at = 30 * (n % 4) + 10 * q + 2
            x = roll(roll(turned[n // 4], 127 - at, 1), 6, 0)
            x = x if n == ED else -x
            b_ref[j] = jnp.where((lane == 127) & (sub >= 6) & last, x, b_ref[j])


def coefficients(v, d, slope, wet):
    return (
        wet * (jnp.maximum(v, 0.0) + d),
        wet * (jnp.minimum(v, 0.0) - d),
        wet * (d * 0.25 * slope),
    )


def tile(t):
    return pl.ds(8 * t, 8)


def rows_up(sub, here, above):
    return jnp.where(sub == 7, roll(above, -1, 0), roll(here, -1, 0))


def rows_down(sub, here, below):
    return jnp.where(sub == 0, roll(below, 1, 0), roll(here, 1, 0))


def north_coefficients(ring, v, d, s, wet, put, far=None):
    sub = iota((8, 128), 0)
    size = len(ring)
    known = {}
    for at in [size - 1] + list(range(size)):
        t = ring[at]
        if t not in known:
            wet_t = wet(t) * rows_up(sub, wet(t), wet(ring[(at + 1) % size]))
            known[t] = coefficients(v(t), d(t), s(t), wet_t)
            if far and t == 15:
                x, y, z = coefficients(*(roll(f, -1, 0) for f in far[:3]), wet_t)
                beyond = jnp.logical_and(far[3], sub == 7)
                a2, b2, c2 = (jnp.where(beyond, f, g) for f, g in zip((x, y, z), known[t]))
                far[4](0, a2)
                far[4](1, c2)
        below = known.get(ring[at - 1])
        if below is not None:
            a, b, c = known[t]
            put(t, 4, a)
            put(t, 5, c)
            put(t, 6, rows_down(sub, b, below[1]))
            put(t, 7, rows_down(sub, c, below[2]))
            if far and t == 16:
                far[4](2, rows_down(sub, b, b2))
                far[4](3, rows_down(sub, c, c2))


def terms(ring, coef, coef2, state, vertical, push, skip=()):
    sub = iota((8, 128), 0)
    size = len(ring)
    held = {}

    def make(t):
        s, u = state(t), vertical(t)
        up_face = coef(t, 4) * s + coef(t, 5) * u
        down_face = coef(t, 6) * s + coef(t, 7) * u
        far, near = up_face, down_face
        if coef2 and t == 15:
            far = coef2(0) * s + coef2(1) * u
        if coef2 and t == 16:
            near = coef2(2) * s + coef2(3) * u
        part = None
        if t not in skip:
            east, west = coef(t, 0) * s + coef(t, 1) * u, coef(t, 2) * s + coef(t, 3) * u
            push(t, east, west)
            part = s + (west - east) + (near - up_face)
        held[t] = part, up_face, far, down_face

    make(ring[-1])
    make(ring[0])
    for at, t in enumerate(ring):
        if at + 1 < size - 1:
            make(ring[at + 1])
        if t in skip:
            continue
        part, up_face, _, down_face = held[t]
        x = rows_down(sub, up_face, held[ring[at - 1]][2])
        y = rows_up(sub, down_face, held[ring[(at + 1) % size]][3])
        yield t, part + (x - y)


def block_kernel(tr, ls, fe, fn, lev_in, out, strip_ref, ends, SA, SB, W, K, D):
    lev, _, _ = position()
    refs = (tr, ls, fe, fn)
    lane = iota((8, 128), 1)
    ring = list(range(16))
    half = jnp.where(lev == 0, 0.5, -0.5)
    zero = jnp.zeros((128, 128), f32)

    for t in ring:
        for i in range(3):
            east = west = jnp.zeros((8, 128), f32)
            for n in range(4 * i, min(4 * i + 4, 9)):
                for q in range(3):
                    x = raw(refs, n, level(q, lev), tile(t))
                    at = 30 * (n % 4) + 10 * q
                    east = jnp.where((lane >= at) & (lane < at + 6), roll(x, at - 122, 1), east)
                    west = jnp.where((lane >= at + 3) & (lane < at + 9), roll(x, at + 3, 1), west)
            strip_ref[0, i, tile(t)] = east
            strip_ref[1, i, tile(t)] = west

    for c in range(2):
        SA[c, 0] = zero
        SB[c, 0] = zero
    W[0] = zero
    for q in range(3):
        kk = level(q, lev)
        for c in range(2):
            SA[c, q + 1] = tr[c, kk]
            SA[c, 6 - q] = lev_in[3 * c + q]
        W[q + 1] = ls[kk].astype(f32)
        W[6 - q] = lev_in[6 + q]

    for q in range(5):
        kk = level(min(q, 2), lev)

        def field(n, t):
            if q >= 3:
                return lev_in[9 + (EV, ED, ES, NV, ND, NS).index(n) * 2 + 4 - q, tile(t)]
            return raw(refs, n, kk, tile(t))

        for t in ring:
            wet = W[q + 1, tile(t)]
            D[0, 0, tile(t)] = wet * roll(wet, -1, 1)
            K[q, 8, tile(t)] = half * W[q, tile(t)] * wet * W[q + 2, tile(t)]
        for t in ring:
            a, b, c = coefficients(field(EV, t), field(ED, t), field(ES, t), D[0, 0, tile(t)])
            K[q, 0, tile(t)] = a
            K[q, 1, tile(t)] = c
            K[q, 2, tile(t)] = roll(b, 1, 1)
            K[q, 3, tile(t)] = roll(c, 1, 1)

        def put(t, at, x):
            K[q, at, tile(t)] = x

        north_coefficients(
            ring, lambda t: field(NV, t), lambda t: field(ND, t), lambda t: field(NS, t),
            lambda t: W[q + 1, tile(t)], put,
        )
        for k in (0, 1, 2, 3, 8):
            ends[q, k, 0] = K[q, k, tile(0)]
            ends[q, k, 1] = K[q, k, tile(15)]

    for step in range(STEPS):
        now, later = (SA, SB) if step % 2 == 0 else (SB, SA)

        @pl.loop(0, 5 - step)
        def _(q):
            for c in range(2):
                def push(t, east, west):
                    D[c, 0, tile(t)] = roll(east, 1, 1)
                    D[c, 1, tile(t)] = roll(west, -1, 1)

                def vertical(t):
                    return K[q, 8, tile(t)] * (now[c, q + 2, tile(t)] - now[c, q, tile(t)])

                for t, part in terms(
                    ring, lambda t, i: K[q, i, tile(t)], None,
                    lambda t: now[c, q + 1, tile(t)], vertical, push,
                ):
                    D[c, 2, tile(t)] = part
            for c in range(2):
                for t in ring:
                    x = D[c, 2, tile(t)] + (D[c, 0, tile(t)] - D[c, 1, tile(t)])
                    if step == STEPS - 1:
                        out[c, level(q, lev), tile(t)] = x
                    else:
                        later[c, q + 1, tile(t)] = x


class Strips:
    def __init__(self, ring, spot, lev):
        self.ring, self.spot = ring, spot
        self.half = jnp.where(lev == 0, 0.5, -0.5)
        lane = iota((8, 128), 1)
        m = lane % 10
        group = lane // 10
        self.second = group >= 6
        self.q = group % 6
        self.mine = self.q < 3
        self.used = (lane < 120) & (m < 9)
        self.index = jnp.where(self.mine, 10 * self.q + m, 10 * (5 - self.q) + m)

    def pick(self, n, own, partner):
        index = self.index + (jnp.where(self.second, 60, 0) if n == S0 else 30 * (n % 4))
        index = jnp.clip(index, 0, 127)
        x = jnp.take_along_axis(own, index, axis=1)
        y = jnp.take_along_axis(partner, index, axis=1)
        return jnp.where(self.used, jnp.where(self.mine, x, y), 0.0)

    def faces(self, side, F, SK, first, D, tiles=None):
        outside = (self.q == 0) | (self.q == 5)
        for t in tiles or self.ring:
            at = self.spot[t]
            wet = F[side, WET, at]
            D[side, 0, at] = wet * roll(wet, -1, 1)
            around = roll(wet, -10, 1) * roll(wet, 10, 1)
            SK[side, 8, at] = jnp.where(outside, 0.0, self.half * wet * around)
            first[side, at] = F[side, S0, at]

    def coefficients(self, side, F, SK, D, far=None, tiles=None):
        for t in tiles or self.ring:
            at = self.spot[t]
            a, b, c = coefficients(*(F[side, n, at] for n in (EV, ED, ES)), D[side, 0, at])
            SK[side, 0, at] = a
            SK[side, 1, at] = c
            SK[side, 2, at] = roll(b, 1, 1)
            SK[side, 3, at] = roll(c, 1, 1)

        def put(t, k, x):
            SK[side, k, self.spot[t]] = x

        north_coefficients(
            self.ring, *(lambda t, n=n: F[side, n, self.spot[t]] for n in (NV, ND, NS, WET)), put, far
        )

    def vertical(self, side, now, SK, U):
        for t in self.ring:
            at = self.spot[t]
            s = now[side, at]
            U[side, at] = SK[side, 8, at] * (roll(s, -10, 1) - roll(s, 10, 1))

    def step(self, side, now, SK, SK2, U, D):
        def push(t, east, west):
            D[side, 0, self.spot[t]] = roll(east, 1, 1)
            D[side, 1, self.spot[t]] = roll(west, -1, 1)

        for t, part in terms(
            self.ring, lambda t, k: SK[side, k, self.spot[t]],
            None if SK2 is None else lambda k: SK2[side, k],
            lambda t: now[side, self.spot[t]], lambda t: U[side, self.spot[t]], push,
        ):
            D[side, 2, self.spot[t]] = part

    def update(self, side, later, D):
        for t in self.ring:
            at = self.spot[t]
            later[side, at] = D[side, 2, at] + (D[side, 0, at] - D[side, 1, at])

    def edge(self, last_strips, at):
        m = iota((8, 128), 1) % 10
        return jnp.where(m < 3, roll(last_strips[0, at], -3, 1), last_strips[1, at])


def strip_prep_kernel(strip_o, strip_p, SK, first, ends, F, D):
    lev, _, _ = position()
    strips = Strips(list(range(16)), {t: tile(t) for t in range(16)}, lev)
    for side in range(2):
        for n in range(9):
            if n != S1:
                for t in range(16):
                    F[side, n, tile(t)] = strips.pick(
                        n, strip_o[side, n // 4, tile(t)], strip_p[side, n // 4, tile(t)]
                    )
    for side in range(2):
        strips.faces(side, F, SK, first, D)
    for side in range(2):
        strips.coefficients(side, F, SK, D)
    for side in range(2):
        for n in range(9):
            if n != S1:
                ends[side, n, 0] = F[side, n, tile(0)]
                ends[side, n, 1] = F[side, n, tile(15)]


def stack_kernel(b, a, _, both):
    both[0] = a[...]
    both[1] = b[...]


def strip_steps_kernel(SK, first, block, _, whole, SA, SB, U, D):
    lev, _, _ = position()
    lane = iota((8, 128), 1)
    strips = Strips(list(range(16)), {t: tile(t) for t in range(16)}, lev)
    now = first
    for step in range(STEPS):
        later = SB if step % 2 else SA
        for side in range(2):
            strips.vertical(side, now, SK, U)
        for side in range(2):
            strips.step(side, now, SK, None, U, D)
        for side in range(2):
            strips.update(side, later, D)
        now = later
    for t in range(16):
        U[0, tile(t)] = strips.edge(now, tile(t))
    for c in range(2):
        for q in range(3):
            kk = level(q, lev)
            for t in range(16):
                edge = roll(U[0, tile(t)], 125 - 10 * (6 * c + q), 1)
                whole[c, kk, tile(t)] = jnp.where((lane < 3) | (lane >= 125), edge, block[c, kk, tile(t)])


def frame_kernel(
    tr, ls, fe, fn, lev_in, most, block_ends, strip_ends, strip_coefs, rows_o, rows_p,
    out, SA, SB, W, K, K2, D, F, SK, SK2, SS0, SS1, U, DS, rims, sem,
):
    lev, odd, last = position()
    refs = (tr, ls, fe, fn)
    lane = iota((8, 128), 1)
    sub = iota((8, 128), 0)
    half = jnp.where(lev == 0, 0.5, -0.5)
    ring = [15, 16, 0]
    spot = {15: pl.ds(0, 8), 16: pl.ds(8, 8), 0: pl.ds(16, 8)}

    def halo(p, partner):
        rows = rows_p if partner else rows_o
        place = SHORT.index(p) if p in SHORT else TALL.index(p) % 12
        x, y = rows[0, place], rows[1, place]
        north, south = jnp.where(odd, y, x), jnp.where(odd, x, y)
        if p in SHORT:
            north, south = roll(north, -6, 0), roll(south, -2, 0)
        elif TALL.index(p) >= 12:
            north, south = roll(north, -3, 0), roll(south, 3, 0)
        return north, jnp.where(sub >= 5, south, 0.0)

    def joined(n, north, south):
        if n in (NV, ND, NS):
            return jnp.where(sub < 2, jnp.where(last, roll(north, -1, 0), north), south)
        return jnp.where(sub < 3, north, south)

    middle = pl.ds(8, 112)
    bulk = pltpu.make_async_copy(most.at[:, :, middle], out.at[:, :, middle], sem.at[2])
    bulk.start()

    zero = jnp.zeros((24, 128), f32)
    for c in range(2):
        SA[c, 0] = zero
        SB[c, 0] = zero
    W[0] = zero
    for q in range(3):
        kk = level(q, lev)
        for t in (15, 0):
            for c in range(2):
                SA[c, q + 1, spot[t]] = tr[c, kk, tile(t)]
                SA[c, 6 - q, spot[t]] = lev_in[3 * c + q, tile(t)]
            W[q + 1, spot[t]] = ls[kk, tile(t)].astype(f32)
            W[6 - q, spot[t]] = lev_in[6 + q, tile(t)]
        for c in range(2):
            SA[c, q + 1, spot[16]] = joined(S0, *halo(3 * (S0, S1)[c] + q, False))
            SA[c, 6 - q, spot[16]] = joined(S0, *halo(3 * (S0, S1)[c] + q, True))
        W[q + 1, spot[16]] = joined(WET, *halo(3 * WET + q, False))
        W[6 - q, spot[16]] = joined(WET, *halo(3 * WET + q, True))

    def rows_coefficients(q):
        partner = q >= 3
        qq = 5 - q if partner else q
        kk = level(qq, lev)

        def field(n, t):
            if t == 16:
                return joined(n, *halo(3 * n + qq, partner))
            if partner:
                return lev_in[9 + (EV, ED, ES, NV, ND, NS).index(n) * 2 + qq - 1, tile(t)]
            return raw(refs, n, kk, tile(t))

        for k in (0, 1, 2, 3, 8):
            K[q, k, spot[0]] = block_ends[q, k, 0]
            K[q, k, spot[15]] = block_ends[q, k, 1]
        a, b, c = coefficients(field(EV, 16), field(ED, 16), field(ES, 16), D[q, 0, 0, spot[16]])
        K[q, 0, spot[16]] = a
        K[q, 1, spot[16]] = c
        K[q, 2, spot[16]] = roll(b, 1, 1)
        K[q, 3, spot[16]] = roll(c, 1, 1)
        K[q, 8, spot[16]] = half * W[q, spot[16]] * W[q + 1, spot[16]] * W[q + 2, spot[16]]

        def put(t, at, x):
            K[q, at, spot[t]] = x

        def put2(at, x):
            K2[q, at] = x

        north_coefficients(
            ring, lambda t: field(NV, t), lambda t: field(ND, t), lambda t: field(NS, t),
            lambda t: W[q + 1, spot[t]], put,
            (*(halo(3 * n + qq, partner)[0] for n in (NV, ND, NS)), last, put2),
        )

    def rows_step(step, q):
        now = SA if step % 2 == 0 else SB
        for c in range(2):
            def push(t, east, west):
                D[q, c, 0, spot[t]] = roll(east, 1, 1)
                D[q, c, 1, spot[t]] = roll(west, -1, 1)

            def vertical(t):
                return K[q, 8, spot[t]] * (now[c, q + 2, spot[t]] - now[c, q, spot[t]])

            for t, part in terms(
                ring, lambda t, i: K[q, i, spot[t]], lambda i: K2[q, i],
                lambda t: now[c, q + 1, spot[t]], vertical, push,
            ):
                D[q, c, 2, spot[t]] = part

    def rows_update(step):
        later = SB if step % 2 == 0 else SA
        for q in range(5 - step):
            for c in range(2):
                later[c, q + 1] = D[q, c, 2] + (D[q, c, 0] - D[q, c, 1])

    strips = Strips(ring, spot, lev)
    far = [[None] * 3, [None] * 3]

    def spread(side):
        for n in range(9):
            if n == S1:
                continue
            i = n // 4
            F[side, n, spot[0]] = strip_ends[side, n, 0]
            F[side, n, spot[15]] = strip_ends[side, n, 1]
            p = 27 + 3 * side + i
            north, south = (strips.pick(n, x, y) for x, y in zip(halo(p, False), halo(p, True)))
            F[side, n, spot[16]] = joined(n, north, south)
            if n in (NV, ND, NS):
                far[side][n - NV] = north
        for t in (0, 15):
            SS0[side, spot[t]] = F[side, S0, spot[t]]
            for k in (0, 1, 2, 3, 8):
                SK[side, k, spot[t]] = strip_coefs[side, k, tile(t)]

    def put_far(side):
        def put(k, x):
            SK2[side, k] = x
        return (*far[side], last, put)

    for q in range(5):
        wet = W[q + 1, spot[16]]
        D[q, 0, 0, spot[16]] = wet * roll(wet, -1, 1)
    for side in range(2):
        spread(side)
    for q in range(5):
        rows_coefficients(q)
    for side in range(2):
        strips.faces(side, F, SK, SS0, DS, [16])
    for side in range(2):
        strips.coefficients(side, F, SK, DS, put_far(side), [16])
    for step in range(STEPS):
        now, later = (SS0, SS1) if step % 2 == 0 else (SS1, SS0)
        for side in range(2):
            strips.vertical(side, now, SK, U)
        for q in range(5 - step):
            rows_step(step, q)
        for side in range(2):
            strips.step(side, now, SK, SK2, U, DS)
        rows_update(step)
        for side in range(2):
            strips.update(side, later, DS)

    rows_last, strips_last = (SB, SS1) if STEPS % 2 else (SA, SS0)
    copies = [bulk]
    for side, t, rim in ((0, 0, sub < 3), (1, 15, sub >= 5)):
        edges = strips.edge(strips_last, spot[t])
        for c in range(2):
            for q in range(3):
                kk = level(q, lev)
                edge = roll(edges, 125 - 10 * (6 * c + q), 1)
                x = jnp.where((lane < 3) | (lane >= 125), edge, rows_last[c, q + 1, spot[t]])
                rims[side, c, kk] = jnp.where(rim, x, most[c, kk, tile(t)])
        copy = pltpu.make_async_copy(rims.at[side], out.at[:, :, tile(t)], sem.at[side])
        copy.start()
        copies.append(copy)
    for copy in copies:
        copy.wait()


PREP_SCRATCH = [(2, 9, 128, 128), (2, 1, 128, 128)]
STRIP_SCRATCH = [(2, 128, 128), (2, 128, 128), (2, 128, 128), (2, 3, 128, 128)]
FRAME_SCRATCH = [
    (2, 7, 24, 128), (2, 7, 24, 128), (7, 24, 128), (5, 9, 24, 128), (5, 4, 8, 128), (5, 2, 3, 24, 128),
    (2, 9, 24, 128), (2, 9, 24, 128), (2, 4, 8, 128), (2, 24, 128), (2, 24, 128), (2, 24, 128), (2, 3, 24, 128),
    (2, 2, 3, 8, 128), pltpu.SemaphoreType.DMA((3,)),
]


def call(kernel, shapes, scratch=(), types=(), in_specs=None, out_specs=None, cost=None):
    types = list(types) + [f32] * (len(shapes) - len(types))
    return pl.pallas_call(
        kernel,
        out_shape=[jax.ShapeDtypeStruct(s, d) for s, d in zip(shapes, types)],
        **({} if in_specs is None else dict(in_specs=in_specs)),
        out_specs=out_specs or [VMEM] * len(shapes),
        scratch_shapes=[pltpu.VMEM(s, f32) if isinstance(s, tuple) else s for s in scratch],
        compiler_params=PARAMS,
        cost_estimate=cost and pl.CostEstimate(flops=cost, bytes_accessed=cost, transcendentals=0),
    )


def local(tracers, land_sea, faces_east, faces_north):
    lons, lats = lax.axis_size("lon"), lax.axis_size("lat")
    swap = [(0, 1), (1, 0)]

    inputs = (tracers, land_sea, faces_east, faces_north)
    hbm = pl.BlockSpec(memory_space=pltpu.HBM)
    *blocks, to_east, to_west = call(
        edges_kernel,
        [x.shape for x in inputs] + [(128, 128), (128, 128)],
        [(3, 128, 128), pltpu.SemaphoreType.DMA((9,))],
        types=[x.dtype for x in inputs],
        in_specs=[hbm] * 4,
    )(*[pltpu.with_memory_space_constraint(x, pltpu.HBM) for x in inputs])
    from_west = lax.ppermute(to_east, "lon", [(i, (i + 1) % lons) for i in range(lons)])
    from_east = lax.ppermute(to_west, "lon", [((i + 1) % lons, i) for i in range(lons)])
    levels, rows_a, rows_b = call(planes_kernel, [(21, 128, 128), (12, 8, 128), (12, 8, 128)])(*blocks)
    lev_in = lax.ppermute(levels, "lev", swap)
    block, strip, block_ends = call(
        block_kernel,
        [(2, 3, 128, 128), (2, 3, 128, 128), (5, 9, 2, 8, 128)],
        [(2, 7, 128, 128), (2, 7, 128, 128), (7, 128, 128), (5, 9, 128, 128), (2, 3, 128, 128)],
        cost=20_000_000,
    )(*blocks, lev_in)
    rows_b, rows_a, full = call(rows_kernel, [(12, 8, 128), (12, 8, 128), (2, 3, 128, 128)])(
        strip, from_east, from_west, rows_a, rows_b
    )

    def at(lon, lat):
        return lon * lats + lat

    route_a, route_b = [], []
    for lon in range(lons):
        for lat in range(lats):
            other = lat + 1 if lat % 2 == 0 else lat - 1
            route_a.append((at(lon, lat), at(lon, other)))
            if lat == lats - 1:
                route_b.append((at(lon, lat), at(lons - 1 - lon, lat)))
            elif lat > 0:
                other = lat - 1 if lat % 2 == 0 else lat + 1
                route_b.append((at(lon, lat), at(lon, other)))
    got_b = lax.ppermute(rows_b, ("lon", "lat"), route_b)
    got_a = lax.ppermute(rows_a, ("lon", "lat"), route_a)
    full_p = lax.ppermute(full, "lev", swap)
    coefs, first, strip_ends = call(
        strip_prep_kernel,
        [(2, 9, 128, 128), (2, 128, 128), (2, 9, 2, 8, 128)],
        PREP_SCRATCH,
        cost=4_000_000,
    )(full, full_p)
    (both,) = call(stack_kernel, [(2, 12, 8, 128)])(got_b, got_a, first)
    both_p = lax.ppermute(both, "lev", swap)
    (most,) = call(strip_steps_kernel, [(2, 3, 128, 128)], STRIP_SCRATCH, cost=6_000_000)(
        coefs, first, block, both
    )
    (out,) = call(frame_kernel, [(2, 3, 128, 128)], FRAME_SCRATCH, out_specs=[hbm])(
        *blocks, lev_in, most, block_ends, strip_ends, coefs, both, both_p
    )
    return out


def solution(mesh):
    return jax.shard_map(
        local,
        mesh=mesh,
        in_specs=(
            P("members", "lev", "lat", "lon"),
            P("lev", "lat", "lon"),
            P("members", "lev", "lat", "lon"),
            P("members", "lev", "lat", "lon"),
        ),
        out_specs=P("members", "lev", "lat", "lon"),
        check_vma=False,
    )
```
